256 devices in a mesh: island: 8 (over z_hi, core), expert: 32 (over y, z_lo, x).
Axes of the slice: x: 4, y: 4, z: 8 (z_hi: 4, z_lo: 2; z = z_hi * 2 + z_lo), core: 2. Of those that a mesh axis runs over, the one named last changes fastest.
Arguments:
- tokens: bfloat16 [32768, 1792], P(('island', 'expert')), may hold values from -6 to 6
- cotangent: bfloat16 [32768, 1792], P(('island', 'expert')), may hold values from -6 to 6
- route_ids: int32 [32768, 2], P(('island', 'expert')), may hold values from 0 to 15, all different within a row; in each aligned block of 128 rows (0 to 127, 128 to 255, ...) at most 20 rows name the same one
- router_gate_weights: float32 [32768, 2], P(('island', 'expert')), may hold values from 0.1 to 1
- w_gate: bfloat16 [14336, 20480], P('island', 'expert'), may hold values from -0.125 to 0.125
- w_up: bfloat16 [14336, 20480], P('island', 'expert'), may hold values from -0.125 to 0.125
- w_down: bfloat16 [163840, 1792], P(('island', 'expert')), may hold values from -0.15625 to 0.15625
- outer_down: float32 [20480, 1792], P('expert', 'island'), may hold values from -0.15625 to 0.15625
- momentum: float32 [20480, 1792], P('expert', 'island'), may hold values from -0.12 to 0.12
Outputs:
- mixed: bfloat16 [32768, 1792], P(('island', 'expert'))
- input_grad: bfloat16 [32768, 1792], P(('island', 'expert'))
- outer_next: float32 [20480, 1792], P('expert', 'island')
- momentum_next: float32 [20480, 1792], P('expert', 'island')
- fresh_down: bfloat16 [20480, 1792], P('expert')
The draws below stay inside these ranges and needn't reach their ends.
Inputs may be any that keep to these rules, and one draw needn't show every extreme that they name: `route_ids`: each row names 2 different experts. In each aligned block of 128 rows (the tokens of one device) no expert is named more than 20 times, and in every draw some expert is named exactly 20 times in some block.
All inputs are finite; a program needn't handle non-finite values.
Results may differ from the reference program's by a relative error of at most 0.0064.
Values may be sent and summed in bfloat16 or wider, within the bound.
No kernel may reach another device: no remote copies, remote signals or barrier semaphores. Data moves between devices by JAX's collectives and lax.ppermute only.
A program may use at most 128 MiB of HBM per device.

```python
import math
import jax
import jax.numpy as jnp
import numpy as np
from jax import lax

DW = 1792
FFW = 1280
SPLIT = 2
TOP = 2
TOK_DEV = 128
HID_DEV = 640
EXPERTS = 16
CAP = 20
TOKENS = 4096
ALL_TOKENS = 32768
N_ISLAND = 8
N_EXPERT = 32


def levels(stream_key, shape, pieces, smallest, top_value):
    def one(dim, shards_of):
        heights = jax.random.uniform(jax.random.fold_in(jax.random.fold_in(stream_key, 6), dim), (shards_of,), jnp.float32, smallest / len(pieces), top_value / len(pieces))
        return jnp.repeat(jnp.exp(heights), shape[dim] // shards_of).reshape((-1,) + (1,) * (len(shape) - dim - 1))

    gain = one(*pieces[0])
    for cut in pieces[1:]:
        gain = gain * one(*cut)
    return gain


def shared_out(key, own, number, rows, count, top, most, slope):
    ranking = jax.random.permutation(key, count)
    crowded, common = shares(count, rows * top, most, slope, True), shares(count, rows * top, most, slope, False)
    places = jnp.arange(count)

    def named(tallies, rotation):
        used = int((tallies > 0).sum())
        fixed = max(1, used // 4)
        shifted = fixed + (places - fixed + rotation * (used - fixed)) % max(1, count - fixed)
        return jnp.zeros((count,), jnp.int32).at[ranking[jnp.where(places < fixed, places, shifted)]].set(jnp.asarray(tallies, jnp.int32))

    tallies = jnp.where(number % 4 == 0, named(crowded, number // 4), named(common, number - number // 4 - 1))
    mixed = jax.random.permutation(jax.random.fold_in(own, 3), count)
    donor, sink = mixed[0:count // 2 * 2:2], mixed[1:count // 2 * 2:2]
    slack = jnp.minimum(tallies[donor] - 1, most - tallies[sink]) // 2
    slack = jnp.where((donor == ranking[0]) | (sink == ranking[0]) | (tallies[sink] == 0), 0, jnp.maximum(slack, 0))
    shifted = jax.random.randint(jax.random.fold_in(own, 4), (count // 2,), 0, 1 << 20) % (slack + 1)
    tallies = tallies.at[donor].add(-shifted).at[sink].add(shifted)
    items = jnp.searchsorted(jnp.cumsum(tallies), jnp.arange(rows * top), side="right").astype(jnp.int32)
    listing = items.reshape(top, rows).T
    listing = listing[jax.random.permutation(jax.random.fold_in(own, 1), rows)]
    rotation = jax.random.randint(jax.random.fold_in(own, 2), (rows, 1), 0, top)
    return jnp.take_along_axis(listing, (jnp.arange(top)[None, :] + rotation) % top, axis=1)


def shares(amount, total, reach, lean, full):
    weights = [(1 << 20) // math.isqrt(rank ** lean) + 1 for rank in range(1, amount + 1)]
    largest = reach if full else min(reach, max(-(-total // amount), total * weights[0] // sum(weights)))
    least = 1 if total - largest >= amount - 1 else 0
    counts, rest = [largest] + [least] * (amount - 1), total - largest - least * (amount - 1)
    while rest > 0:
        candidates = [i for i in range(1, amount) if counts[i] < largest] or [i for i in range(1, amount) if counts[i] < reach]
        whole, budget = sum([weights[i] for i in candidates]), rest
        for i in candidates:
            extra = min(reach - counts[i], max(1, budget * weights[i] // whole), rest)
            counts[i] = counts[i] + extra
            rest = rest - extra
    return np.array(counts)


def centred(stream_key, shape, scale, reach, pieces=(), held_as=jnp.bfloat16):
    drawn = jax.random.normal(stream_key, shape, jnp.float32) * scale
    if len(pieces) > 0:
        drawn = levels(stream_key, shape, pieces, -0.22, 0.18) * drawn
    return jnp.clip(drawn, min=-reach, max=reach).astype(held_as)


def setup_inputs(seed: int = 0) -> dict:
    keys = jax.random.split(jax.random.key(seed), 10)
    tokens = centred(keys[0], (ALL_TOKENS, DW), 1.0, 6.0, ((0, 256),))
    cotangent = centred(keys[1], (ALL_TOKENS, DW), 1.0, 6.0, ((0, 256),))
    route_ids_keys = jax.random.split(jax.random.fold_in(keys[2], 1), ALL_TOKENS // TOK_DEV)
    route_ids_turns = jax.random.permutation(jax.random.fold_in(keys[2], 3), ALL_TOKENS // TOK_DEV)
    route_ids = jax.vmap(lambda own, number: shared_out(jax.random.fold_in(keys[2], 2), own, number, TOK_DEV, EXPERTS, TOP, CAP, 2))(route_ids_keys, route_ids_turns).reshape((ALL_TOKENS, TOP))
    router_gate_weights = jnp.clip(0.1 + 0.9 * jax.random.uniform(keys[3], (ALL_TOKENS, TOP), jnp.float32) ** levels(keys[3], (ALL_TOKENS, TOP), ((0, 256),), -0.2, 0.2), 0.1, 1.0)
    w_gate = centred(keys[4], (N_ISLAND * DW, EXPERTS * FFW), DW ** -0.5, 0.125, ((0, 8), (1, 32)))
    w_up = centred(keys[5], (N_ISLAND * DW, EXPERTS * FFW), DW ** -0.5, 0.125, ((0, 8), (1, 32)))
    w_down = centred(keys[6], (N_ISLAND * EXPERTS * FFW, DW), FFW ** -0.5, 0.15625, ((0, 256),))
    outer_down = centred(keys[7], (EXPERTS * FFW, DW), FFW ** -0.5, 0.15625, ((0, 32), (1, 8)), jnp.float32)
    momentum = centred(keys[8], (EXPERTS * FFW, DW), 0.02, 0.12, ((0, 32), (1, 8)), jnp.float32)
    return {"tokens": tokens, "cotangent": cotangent, "route_ids": route_ids, "router_gate_weights": router_gate_weights, "w_gate": w_gate, "w_up": w_up, "w_down": w_down, "outer_down": outer_down, "momentum": momentum}


inner_rate = 0.001
outer_rate = 0.7
outer_beta = 0.9


def slot_index(block_routes, expert_count, capacity):
    flat_ids = block_routes.reshape(-1).astype(jnp.int32)
    one_hot = (flat_ids[:, None] == jnp.arange(expert_count, dtype=jnp.int32)[None, :]).astype(jnp.int32)
    before = jnp.cumsum(one_hot, axis=0) - one_hot
    slot_number = jnp.sum(before * one_hot, axis=1).astype(jnp.int32)
    return (flat_ids * capacity + slot_number).astype(jnp.int32)


def expert_shard(rows_x, rows_s, gate_cols, up_cols, down_rows):
    dims_last = (((1,), (1,)), ((), ()))
    dims_first = (((0,), (0,)), ((), ()))
    gate_pre = jnp.dot(rows_x, gate_cols, preferred_element_type=jnp.float32)
    up_pre = jnp.dot(rows_x, up_cols, preferred_element_type=jnp.float32)
    sigmoid_a = jax.nn.sigmoid(gate_pre)
    activated = gate_pre * sigmoid_a
    hidden = (activated * up_pre).astype(jnp.bfloat16)
    part_output = jnp.dot(hidden, down_rows, preferred_element_type=jnp.float32).astype(jnp.bfloat16)
    grad_hidden = lax.dot_general(rows_s, down_rows, dims_last, preferred_element_type=jnp.float32)
    grad_down = lax.dot_general(hidden, rows_s, dims_first, preferred_element_type=jnp.float32)
    grad_gate = (grad_hidden * up_pre * sigmoid_a * (1.0 + gate_pre * (1.0 - sigmoid_a))).astype(jnp.bfloat16)
    grad_up = (grad_hidden * activated).astype(jnp.bfloat16)
    part_input = (lax.dot_general(grad_gate, gate_cols, dims_last, preferred_element_type=jnp.float32)
                  + lax.dot_general(grad_up, up_cols, dims_last, preferred_element_type=jnp.float32)).astype(jnp.bfloat16)
    return part_output, part_input, grad_down


def reference(tokens, cotangent, route_ids, router_gate_weights, w_gate, w_up, w_down, outer_down, momentum):
    row_count = N_EXPERT * CAP
    picks_num = TOK_DEV * TOP

    def island_step(inputs):
        x_island, s_island, routes, gates, gate_all, up_all, down_all = inputs
        token_blocks = x_island.reshape(N_EXPERT, TOK_DEV, DW)
        cot_blocks = s_island.reshape(N_EXPERT, TOK_DEV, DW)
        gate_blocks = gates.reshape(N_EXPERT, TOK_DEV, TOP)
        targets = jax.vmap(lambda block_routes: slot_index(block_routes, EXPERTS, CAP))(
            routes.reshape(N_EXPERT, TOK_DEV, TOP))
        chosen_tokens = jnp.broadcast_to(token_blocks[:, :, None, :], (N_EXPERT, TOK_DEV, TOP, DW)).reshape(N_EXPERT, picks_num, DW)
        chosen_scores = (gate_blocks[..., None] * cot_blocks[:, :, None, :].astype(jnp.float32)).astype(jnp.bfloat16)
        chosen_scores = chosen_scores.reshape(N_EXPERT, picks_num, DW)
        slot_assignment = (targets[:, None, :] == jnp.arange(EXPERTS * CAP, dtype=jnp.int32)[None, :, None]).astype(jnp.float32)
        slot_buffer_tokens = jnp.einsum('lve,lec->lvc', slot_assignment, chosen_tokens.astype(jnp.float32)).astype(jnp.bfloat16)
        slot_buffer_scores = jnp.einsum('lve,lec->lvc', slot_assignment, chosen_scores.astype(jnp.float32)).astype(jnp.bfloat16)
        slot_buffer_tokens = slot_buffer_tokens.reshape(N_EXPERT, EXPERTS, CAP, DW)
        slot_buffer_scores = slot_buffer_scores.reshape(N_EXPERT, EXPERTS, CAP, DW)

        def shard_step(shard_id):
            expert_id = shard_id // SPLIT
            rows_x = lax.dynamic_index_in_dim(slot_buffer_tokens, expert_id, axis=1, keepdims=False).reshape(row_count, DW)
            rows_s = lax.dynamic_index_in_dim(slot_buffer_scores, expert_id, axis=1, keepdims=False).reshape(row_count, DW)
            start = (shard_id * HID_DEV).astype(jnp.int32)
            gate_cols = lax.dynamic_slice_in_dim(gate_all, start, HID_DEV, 1)
            up_cols = lax.dynamic_slice_in_dim(up_all, start, HID_DEV, 1)
            down_rows = lax.dynamic_slice_in_dim(down_all, start, HID_DEV, 0)
            return expert_shard(rows_x, rows_s, gate_cols, up_cols, down_rows)

        part_output, part_input, grad_down = lax.map(shard_step, jnp.arange(N_EXPERT, dtype=jnp.int32))

        def combine_parts(parts):
            summed = parts.reshape(EXPERTS, SPLIT, N_EXPERT, CAP, DW).astype(jnp.float32).sum(axis=1)
            summed = jnp.transpose(summed, (1, 0, 2, 3)).reshape(N_EXPERT, EXPERTS * CAP, DW)
            picked = jnp.take_along_axis(summed, targets[:, :, None], axis=1)
            return picked.reshape(N_EXPERT, TOK_DEV, TOP, DW)

        mixed = jnp.sum(gate_blocks[..., None] * combine_parts(part_output), axis=2).astype(jnp.bfloat16)
        input_grad = jnp.sum(combine_parts(part_input), axis=2).astype(jnp.bfloat16)
        inner_new = down_all.astype(jnp.float32) - inner_rate * grad_down.reshape(EXPERTS * FFW, DW)
        return mixed.reshape(TOKENS, DW), input_grad.reshape(TOKENS, DW), inner_new

    stacked = (tokens.reshape(N_ISLAND, TOKENS, DW), cotangent.reshape(N_ISLAND, TOKENS, DW),
               route_ids.reshape(N_ISLAND, TOKENS, TOP), router_gate_weights.reshape(N_ISLAND, TOKENS, TOP),
               w_gate.reshape(N_ISLAND, DW, EXPERTS * FFW), w_up.reshape(N_ISLAND, DW, EXPERTS * FFW),
               w_down.reshape(N_ISLAND, EXPERTS * FFW, DW))
    mixed, input_grad, inner_all = lax.map(island_step, stacked)
    mean_delta = outer_down - jnp.sum(inner_all, axis=0) / N_ISLAND
    momentum_next = outer_beta * momentum + mean_delta
    outer_next = outer_down - outer_rate * (mean_delta + outer_beta * momentum_next)
    fresh_down = outer_next.astype(jnp.bfloat16)
    return (mixed.reshape(ALL_TOKENS, DW), input_grad.reshape(ALL_TOKENS, DW),
            outer_next, momentum_next, fresh_down)
```

```python
import functools

import jax
import jax.numpy as jnp
from jax import lax
from jax.experimental import pallas as pl
from jax.experimental.pallas import tpu as pltpu
from jax.sharding import PartitionSpec as P

NX = 4
N_YZ = 8
CORES = 2
NZ = 4

inner_rate = 0.001
outer_rate = 0.7
outer_beta = 0.9

F32 = jnp.float32
BF16 = jnp.bfloat16
FIRST = (((0,), (0,)), ((), ()))
LAST = (((1,), (1,)), ((), ()))

VMEM = pl.BlockSpec(memory_space=pltpu.VMEM)
SMEM = pl.BlockSpec(memory_space=pltpu.SMEM)


def call(kernel, out_shape, in_specs, scratch=(), name=None):
    return pl.pallas_call(
        kernel,
        out_shape=out_shape,
        in_specs=in_specs,
        out_specs=jax.tree.map(lambda _: VMEM, out_shape),
        scratch_shapes=scratch,
        compiler_params=pltpu.CompilerParams(vmem_limit_bytes=60 * 1024 * 1024),
        name=name,
    )


def shape(rows, columns, dtype):
    return jax.ShapeDtypeStruct((rows, columns), dtype)


def pick_masks(route, xp, capacity):
    tokens = route.shape[0]
    slots = 2 * N_YZ * capacity
    first, second = route[:, 0:1], route[:, 1:2]
    lane = lax.broadcasted_iota(jnp.int32, (tokens, 128), 1)
    named = ((lane == first) | (lane == second)).astype(BF16)
    earlier = (
        lax.broadcasted_iota(jnp.int32, (tokens, tokens), 1)
        < lax.broadcasted_iota(jnp.int32, (tokens, tokens), 0)
    ).astype(BF16)
    before = jnp.dot(earlier, named, preferred_element_type=F32)
    where = lax.broadcasted_iota(jnp.int32, (tokens, slots), 1)

    def mask(ids):
        slot = jnp.sum(jnp.where(lane == ids, before, 0.0), axis=1, keepdims=True).astype(jnp.int32)
        place = (ids >> 1) * (2 * capacity) + jnp.where((ids & 1) == xp, 0, capacity) + slot
        return where == place

    return mask(first), mask(second)


def as_bf16(mask):
    return jnp.where(mask, 1.0, 0.0).astype(BF16)


def pack_tokens(capacity, half_ref, route_ref, tokens_ref, out_ref):
    one, two = pick_masks(route_ref[...], half_ref[0], capacity)
    chosen = lax.dot_general(as_bf16(one | two), tokens_ref[...], FIRST, preferred_element_type=F32)
    out_ref[...] = chosen.astype(BF16)


def pack_scores(capacity, half_ref, route_ref, gate_ref, cotangent_ref, out_ref):
    one, two = pick_masks(route_ref[...], half_ref[0], capacity)
    lane = lax.broadcasted_iota(jnp.int32, (route_ref.shape[0], 128), 1)

    def parts(column):
        top = column.astype(BF16)
        rest = column - top.astype(F32)
        middle = rest.astype(BF16)
        low = (rest - middle.astype(F32)).astype(BF16)
        return jnp.where(
            lane == 0, top.astype(F32), jnp.where(lane == 1, middle.astype(F32), jnp.where(lane == 2, low.astype(F32), 0.0))
        ).astype(BF16)

    gates = gate_ref[...]
    split = lax.dot_general(as_bf16(one), parts(gates[:, 0:1]), FIRST, preferred_element_type=F32) + lax.dot_general(
        as_bf16(two), parts(gates[:, 1:2]), FIRST, preferred_element_type=F32
    )
    weight = split[:, 0:1] + split[:, 1:2] + split[:, 2:3]
    chosen = lax.dot_general(as_bf16(one | two), cotangent_ref[...], FIRST, preferred_element_type=F32)
    out_ref[...] = (weight * chosen).astype(BF16)


def split_rows(capacity, got_ref, own_ref, other_ref):
    for b in range(N_YZ):
        rows = pl.ds(b * capacity, capacity)
        own_ref[rows, :] = got_ref[pl.ds(2 * b * capacity, capacity), :]
        other_ref[rows, :] = got_ref[pl.ds((2 * b + 1) * capacity, capacity), :]


def merge_rows(capacity, mine_ref, theirs_ref, other_ref, out_ref):
    for b in range(N_YZ):
        rows = pl.ds(b * capacity, capacity)
        whole = mine_ref[rows, :].astype(F32) + theirs_ref[rows, :].astype(F32)
        out_ref[pl.ds(2 * b * capacity, capacity), :] = whole.astype(BF16)
        out_ref[pl.ds((2 * b + 1) * capacity, capacity), :] = other_ref[rows, :]


def forward(x0, x1, x2, x3, gate_ref, up_ref, down_ref, hidden_ref, slope_ref, act_ref, o0, o1, o2, o3):
    rows = x0.shape[0]
    for c, (x, out) in enumerate(((x3, o3), (x2, o2), (x0, o0), (x1, o1))):
        chunk = pl.ds((3, 2, 0, 1)[c] * rows, rows)
        block = x[...]
        gate_pre = jnp.dot(block, gate_ref[...], preferred_element_type=F32)
        up_pre = jnp.dot(block, up_ref[...], preferred_element_type=F32)
        sigmoid_a = jax.nn.sigmoid(gate_pre)
        activated = gate_pre * sigmoid_a
        hidden = (activated * up_pre).astype(BF16)
        hidden_ref[chunk, :] = hidden
        slope_ref[chunk, :] = up_pre * sigmoid_a * (1.0 + gate_pre * (1.0 - sigmoid_a))
        act_ref[chunk, :] = activated
        out[...] = jnp.dot(hidden, down_ref[...], preferred_element_type=F32).astype(BF16)


def backward(s0, s1, s2, s3, gate_ref, up_ref, down_ref, slope_ref, act_ref, o0, o1, o2, o3):
    rows = s0.shape[0]
    for c, (s, out) in enumerate(((s0, o0), (s1, o1), (s2, o2), (s3, o3))):
        chunk = pl.ds(c * rows, rows)
        grad_hidden = lax.dot_general(s[...], down_ref[...], LAST, preferred_element_type=F32)
        grad_gate = (grad_hidden * slope_ref[chunk, :]).astype(BF16)
        grad_up = (grad_hidden * act_ref[chunk, :]).astype(BF16)
        out[...] = (
            lax.dot_general(grad_gate, gate_ref[...], LAST, preferred_element_type=F32)
            + lax.dot_general(grad_up, up_ref[...], LAST, preferred_element_type=F32)
        ).astype(BF16)


def inner_step(place_ref, s0, s1, s2, s3, hidden_ref, down_ref, mine_ref, theirs_ref, whole_ref):
    rows = s0.shape[0]
    total = None
    for c, s in enumerate((s0, s1, s2, s3)):
        part = lax.dot_general(s[...], hidden_ref[pl.ds(c * rows, rows), :], FIRST, preferred_element_type=F32)
        total = part if total is None else total + part
    whole_ref[...] = down_ref[...].astype(F32).T - inner_rate * total
    block = mine_ref.shape[0] // NZ
    z, core = place_ref[0], place_ref[1]
    for d in range(NZ):
        at = lax.rem(z + d, NZ) * CORES
        mine_ref[pl.ds(d * block, block), :] = whole_ref[pl.ds(pl.multiple_of((at + core) * block, 8), block), :]
        theirs_ref[pl.ds(d * block, block), :] = whole_ref[
            pl.ds(pl.multiple_of((at + 1 - core) * block, 8), block), :
        ].astype(BF16)


def outer_step(islands, own_ref, left_ref, right_ref, outer_ref, momentum_ref, next_ref, moved_ref, fresh_ref):
    total = own_ref[...] + left_ref[...].astype(F32) + right_ref[...].astype(F32)
    outer_down = outer_ref[...]
    mean_delta = outer_down - total.T / islands
    momentum_next = outer_beta * momentum_ref[...] + mean_delta
    outer_next = outer_down - outer_rate * (mean_delta + outer_beta * momentum_next)
    next_ref[...] = outer_next
    moved_ref[...] = momentum_next
    fresh_ref[...] = outer_next.T.astype(BF16)


def assemble(place_ref, *refs):
    *parts, out_ref, whole_ref = refs
    z, core = place_ref[0], place_ref[1]
    block = parts[0].shape[0]
    for side in range(CORES):
        own, after, low, high, before = parts[5 * side : 5 * side + 5]
        column = core if side == 0 else 1 - core

        def start(d):
            return pl.multiple_of((lax.rem(z + d, NZ) * CORES + column) * block, 16)

        whole_ref[pl.ds(start(0), block), :] = own[...].astype(F32)
        whole_ref[pl.ds(start(1), block), :] = after[...].astype(F32)
        whole_ref[pl.ds(start(2), block // 2), :] = low[...].astype(F32)
        whole_ref[pl.ds(start(2) + block // 2, block // 2), :] = high[...].astype(F32)
        whole_ref[pl.ds(start(3), block), :] = before[...].astype(F32)
    out_ref[...] = whole_ref[...].T.astype(BF16)


def mix(capacity, half_ref, route_ref, gate_ref, rows_ref, out_ref):
    one, two = pick_masks(route_ref[...], half_ref[0], capacity)
    gates = gate_ref[...]
    rows = rows_ref[...]
    out_ref[...] = (
        gates[:, 0:1] * jnp.dot(as_bf16(one), rows, preferred_element_type=F32)
        + gates[:, 1:2] * jnp.dot(as_bf16(two), rows, preferred_element_type=F32)
    ).astype(BF16)


def gather_grad(capacity, half_ref, route_ref, rows_ref, out_ref):
    one, two = pick_masks(route_ref[...], half_ref[0], capacity)
    out_ref[...] = jnp.dot(as_bf16(one | two), rows_ref[...], preferred_element_type=F32).astype(BF16)


def per_device(tokens, cotangent, route_ids, gates, w_gate, w_up, w_down, outer_down, momentum):
    groups = lax.axis_size("expert")
    islands = lax.axis_size("island")
    token_count, top_count = route_ids.shape
    features = tokens.shape[1]
    hidden_count = w_gate.shape[1]
    experts = groups // 2
    capacity = 5 * token_count * top_count // (4 * experts)
    slots = experts * capacity
    half_rows = slots // 2
    column_count = outer_down.shape[1]

    place = lax.axis_index("expert")
    island = lax.axis_index("island")
    xp = ((place % NX) // 2).astype(jnp.int32).reshape(1)
    at = jnp.stack([island // CORES, island % CORES]).astype(jnp.int32)

    pair = [(i, i ^ 1) for i in range(groups)]
    across = [(i, i ^ 3) for i in range(groups)]
    same_x = [[b * NX + x for b in range(N_YZ)] for x in range(NX)]
    other_core = [(i, i ^ 1) for i in range(islands)]
    ahead = [(i, (i + CORES) % islands) for i in range(islands)]
    behind = [(i, (i - CORES) % islands) for i in range(islands)]

    def to_pair(v):
        return lax.ppermute(v, "expert", pair)

    def to_across(v):
        return lax.ppermute(v, "expert", across)

    def exchange(v):
        v = v.reshape(N_YZ, 2 * capacity, features)
        v = lax.all_to_all(v, "expert", split_axis=0, concat_axis=0, tiled=True, axis_index_groups=same_x)
        return v.reshape(slots, features)

    rows_shape = shape(half_rows, features, BF16)

    def dispatch(packed):
        own, other = call(
            functools.partial(split_rows, capacity), (rows_shape, rows_shape), [VMEM], name="split_rows"
        )(exchange(packed))
        crossed = to_across(other)
        return own, crossed, to_pair(own), to_pair(crossed)

    packed_x = call(
        functools.partial(pack_tokens, capacity), shape(slots, features, BF16), [SMEM, VMEM, VMEM], name="pack_tokens"
    )(xp, route_ids, tokens)
    packed_s = call(
        functools.partial(pack_scores, capacity),
        shape(slots, features, BF16),
        [SMEM, VMEM, VMEM, VMEM],
        name="pack_scores",
    )(xp, route_ids, gates, cotangent)
    xs = dispatch(packed_x)
    ss = dispatch(packed_s)

    total_rows = 2 * slots
    hidden, slope, activated, *outs = call(
        forward,
        (
            shape(total_rows, hidden_count, BF16),
            shape(total_rows, hidden_count, F32),
            shape(total_rows, hidden_count, F32),
        )
        + (rows_shape,) * 4,
        [VMEM] * 7,
        name="forward",
    )(*xs, w_gate, w_up, w_down)

    half_features = CORES * column_count * NZ // 2
    mine, theirs = call(
        inner_step,
        (shape(half_features, hidden_count, F32), shape(half_features, hidden_count, BF16)),
        [SMEM] + [VMEM] * 6,
        scratch=[pltpu.VMEM((features, hidden_count), F32)],
        name="inner_step",
    )(at, *ss, hidden, w_down)

    ins = call(backward, (rows_shape,) * 4, [VMEM] * 9, name="backward")(*ss, w_gate, w_up, w_down, slope, activated)

    def give_back(parts):
        own, crossed, pair_own, pair_crossed = parts
        theirs = to_pair(pair_crossed)
        crossed = (crossed.astype(F32) + theirs.astype(F32)).astype(BF16)
        other = to_across(crossed)
        merged = call(
            functools.partial(merge_rows, capacity), shape(slots, features, BF16), [VMEM] * 3, name="merge_rows"
        )(own, to_pair(pair_own), other)
        return exchange(merged)

    back_out = give_back(outs)
    back_in = give_back(ins)
    mixed = call(
        functools.partial(mix, capacity),
        shape(token_count, features, BF16),
        [SMEM] + [VMEM] * 3,
        name="mix",
    )(xp, route_ids, gates, back_out)
    input_grad = call(
        functools.partial(gather_grad, capacity),
        shape(token_count, features, BF16),
        [SMEM] + [VMEM] * 2,
        name="gather_grad",
    )(xp, route_ids, back_in)

    def by_z(v, perm):
        return lax.ppermute(v, "island", perm)

    n = column_count
    h = n // 2
    summed = mine + by_z(theirs, other_core).astype(F32)
    far_low = by_z(summed[2 * n : 2 * n + h].astype(BF16), ahead).astype(F32)
    far_high = by_z(summed[2 * n + h : 3 * n].astype(BF16), behind).astype(F32)
    to_next = jnp.concatenate([summed[n : n + h] + far_low, summed[n + h : 2 * n]]).astype(BF16)
    to_last = jnp.concatenate([summed[3 * n : 3 * n + h], summed[3 * n + h :] + far_high]).astype(BF16)
    from_left = by_z(to_next, ahead)
    from_right = by_z(to_last, behind)
    outer_next, momentum_next, fresh = call(
        functools.partial(outer_step, islands),
        (shape(hidden_count, n, F32), shape(hidden_count, n, F32), shape(n, hidden_count, BF16)),
        [VMEM] * 5,
        name="outer_step",
    )(summed[:n], from_left, from_right, outer_down, momentum)
    left = by_z(fresh, ahead)
    right = by_z(fresh, behind)
    low = by_z(left[:h], ahead)
    high = by_z(right[h:], behind)
    blocks = [fresh, right, low, high, left]
    blocks += [by_z(b, other_core) for b in blocks]
    fresh_down = call(
        assemble,
        shape(hidden_count, features, BF16),
        [SMEM] + [VMEM] * 10,
        scratch=[pltpu.VMEM((features, hidden_count), F32)],
        name="assemble",
    )(at, *blocks)
    return mixed, input_grad, outer_next, momentum_next, fresh_down


def solution(mesh):
    rows = P(("island", "expert"), None)
    columns = P("expert", "island")
    return jax.shard_map(
        per_device,
        mesh=mesh,
        in_specs=(rows, rows, rows, rows, P("island", "expert"), P("island", "expert"), rows, columns, columns),
        out_specs=(rows, rows, columns, columns, P("expert", None)),
        check_vma=False,
    )
```

```python
import functools

import jax
import jax.numpy as jnp
from jax import lax
from jax.experimental import pallas as pl
from jax.experimental.pallas import tpu as pltpu
from jax.sharding import PartitionSpec as P

NX = 4
N_YZ = 8
CORES = 2
NZ = 4

inner_rate = 0.001
outer_rate = 0.7
outer_beta = 0.9

F32 = jnp.float32
BF16 = jnp.bfloat16
FIRST = (((0,), (0,)), ((), ()))
LAST = (((1,), (1,)), ((), ()))

VMEM = pl.BlockSpec(memory_space=pltpu.VMEM)
SMEM = pl.BlockSpec(memory_space=pltpu.SMEM)


def call(kernel, out_shape, args, smem=0, after=(), scratch=(), name=None):
    args, after = list(args), list(after)
    count, skipped = len(args), len(after)

    def body(*refs):
        kernel(*refs[:count], *refs[count + skipped :])

    return pl.pallas_call(
        body,
        out_shape=out_shape,
        in_specs=[SMEM] * smem + [VMEM] * (count - smem) + [pl.BlockSpec(memory_space=pl.ANY)] * skipped,
        out_specs=jax.tree.map(lambda _: VMEM, out_shape),
        scratch_shapes=scratch,
        compiler_params=pltpu.CompilerParams(vmem_limit_bytes=60 * 1024 * 1024),
        name=name,
    )(*args, *after)


def shape(rows, columns, dtype):
    return jax.ShapeDtypeStruct((rows, columns), dtype)


def pick_masks(routes, xp, capacity):
    tokens = routes.shape[1]
    slots = 2 * N_YZ * capacity
    first, second = routes[0:1, :], routes[1:2, :]
    expert = lax.broadcasted_iota(jnp.int32, (2 * N_YZ, tokens), 0)
    named = ((expert == first) | (expert == second)).astype(BF16)
    earlier = (
        lax.broadcasted_iota(jnp.int32, (tokens, tokens), 0)
        < lax.broadcasted_iota(jnp.int32, (tokens, tokens), 1)
    ).astype(BF16)
    before = jnp.dot(named, earlier, preferred_element_type=F32)
    where = lax.broadcasted_iota(jnp.int32, (slots, tokens), 0)

    def mask(ids):
        slot = jnp.sum(jnp.where(expert == ids, before, 0.0), axis=0, keepdims=True).astype(jnp.int32)
        place = (ids >> 1) * (2 * capacity) + jnp.where((ids & 1) == xp, 0, capacity) + slot
        return where == place

    return mask(first), mask(second)


def as_bf16(mask):
    return jnp.where(mask, 1.0, 0.0).astype(BF16)


def pack_tokens(capacity, half_ref, route_ref, tokens_ref, out_ref):
    one, two = pick_masks(route_ref[...], half_ref[0], capacity)
    chosen = jnp.dot(as_bf16(one | two), tokens_ref[...], preferred_element_type=F32)
    out_ref[...] = chosen.astype(BF16)


def pack_scores(capacity, half_ref, route_ref, gate_ref, cotangent_ref, out_ref):
    one, two = pick_masks(route_ref[...], half_ref[0], capacity)
    gates = gate_ref[...]
    weights = jnp.where(one, gates[0:1, :], 0.0) + jnp.where(two, gates[1:2, :], 0.0)
    weight = jnp.sum(weights, axis=1, keepdims=True)
    chosen = jnp.dot(as_bf16(one | two), cotangent_ref[...], preferred_element_type=F32)
    out_ref[...] = (weight * chosen).astype(BF16)


def split_rows(capacity, got_ref, own_ref, other_ref):
    for b in range(N_YZ):
        rows = pl.ds(b * capacity, capacity)
        own_ref[rows, :] = got_ref[pl.ds(2 * b * capacity, capacity), :]
        other_ref[rows, :] = got_ref[pl.ds((2 * b + 1) * capacity, capacity), :]


def merge_rows(capacity, mine_ref, theirs_ref, other_ref, out_ref):
    for b in range(N_YZ):
        rows = pl.ds(b * capacity, capacity)
        whole = mine_ref[rows, :].astype(F32) + theirs_ref[rows, :].astype(F32)
        out_ref[pl.ds(2 * b * capacity, capacity), :] = whole.astype(BF16)
        out_ref[pl.ds((2 * b + 1) * capacity, capacity), :] = other_ref[rows, :]


def add_rows(mine_ref, theirs_ref, out_ref):
    out_ref[...] = (mine_ref[...].astype(F32) + theirs_ref[...].astype(F32)).astype(BF16)


def forward(x0, x1, x2, x3, gate_ref, up_ref, hidden_ref, slope_ref, act_ref):
    rows = x0.shape[0]
    for c, x in enumerate((x0, x1, x2, x3)):
        chunk = pl.ds(c * rows, rows)
        block = x[...]
        gate_pre = jnp.dot(block, gate_ref[...], preferred_element_type=F32)
        up_pre = jnp.dot(block, up_ref[...], preferred_element_type=F32)
        sigmoid_a = jax.nn.sigmoid(gate_pre)
        activated = gate_pre * sigmoid_a
        hidden_ref[chunk, :] = (activated * up_pre).astype(BF16)
        slope_ref[chunk, :] = up_pre * sigmoid_a * (1.0 + gate_pre * (1.0 - sigmoid_a))
        act_ref[chunk, :] = activated


def down(hidden_ref, down_ref, o0, o1, o2, o3):
    rows = o0.shape[0]
    for c, out in enumerate((o0, o1, o2, o3)):
        block = hidden_ref[pl.ds(c * rows, rows), :]
        out[...] = jnp.dot(block, down_ref[...], preferred_element_type=F32).astype(BF16)


def backward(first, s0, s1, gate_ref, up_ref, down_ref, slope_ref, act_ref, o0, o1):
    rows = s0.shape[0]
    for c, (s, out) in enumerate(((s0, o0), (s1, o1))):
        chunk = pl.ds((first + c) * rows, rows)
        grad_hidden = lax.dot_general(s[...], down_ref[...], LAST, preferred_element_type=F32)
        grad_gate = (grad_hidden * slope_ref[chunk, :]).astype(BF16)
        grad_up = (grad_hidden * act_ref[chunk, :]).astype(BF16)
        out[...] = (
            lax.dot_general(grad_gate, gate_ref[...], LAST, preferred_element_type=F32)
            + lax.dot_general(grad_up, up_ref[...], LAST, preferred_element_type=F32)
        ).astype(BF16)


def inner_step(place_ref, s0, s1, s2, s3, hidden_ref, down_ref, mine_ref, theirs_ref, whole_ref):
    rows = s0.shape[0]
    total = None
    for c, s in enumerate((s0, s1, s2, s3)):
        part = lax.dot_general(s[...], hidden_ref[pl.ds(c * rows, rows), :], FIRST, preferred_element_type=F32)
        total = part if total is None else total + part
    whole_ref[...] = down_ref[...].astype(F32).T - inner_rate * total
    block = mine_ref.shape[0] // NZ
    z, core = place_ref[0], place_ref[1]
    for d in range(NZ):
        at = lax.rem(z + d, NZ) * CORES
        mine_ref[pl.ds(d * block, block), :] = whole_ref[pl.ds(pl.multiple_of((at + core) * block, 8), block), :]
        theirs_ref[pl.ds(d * block, block), :] = whole_ref[
            pl.ds(pl.multiple_of((at + 1 - core) * block, 8), block), :
        ].astype(BF16)


def core_sum(mine_ref, theirs_ref, own_ref, before_ref, after_ref, far_low_ref, far_high_ref):
    block = own_ref.shape[0]
    half = block // 2

    def total(start, count):
        rows = pl.ds(start, count)
        return mine_ref[rows, :] + theirs_ref[rows, :].astype(F32)

    own_ref[...] = total(0, block)
    after_ref[...] = total(block, block)
    far_low_ref[...] = total(2 * block, half).astype(BF16)
    far_high_ref[...] = total(2 * block + half, half).astype(BF16)
    before_ref[...] = total(3 * block, block)


def ring_sum(before_ref, after_ref, low_ref, high_ref, to_next_ref, to_last_ref):
    half = low_ref.shape[0]
    low, high = pl.ds(0, half), pl.ds(half, half)
    to_next_ref[low, :] = (after_ref[low, :] + low_ref[...].astype(F32)).astype(BF16)
    to_next_ref[high, :] = after_ref[high, :].astype(BF16)
    to_last_ref[low, :] = before_ref[low, :].astype(BF16)
    to_last_ref[high, :] = (before_ref[high, :] + high_ref[...].astype(F32)).astype(BF16)


def outer_step(islands, own_ref, left_ref, right_ref, outer_ref, momentum_ref, next_ref, moved_ref, fresh_ref):
    total = own_ref[...] + left_ref[...].astype(F32) + right_ref[...].astype(F32)
    outer_down = outer_ref[...]
    mean_delta = outer_down - total.T / islands
    momentum_next = outer_beta * momentum_ref[...] + mean_delta
    outer_next = outer_down - outer_rate * (mean_delta + outer_beta * momentum_next)
    next_ref[...] = outer_next
    moved_ref[...] = momentum_next
    fresh_ref[...] = outer_next.T.astype(BF16)


def assemble(place_ref, *refs):
    *parts, out_ref, whole_ref = refs
    z, core = place_ref[0], place_ref[1]
    block = parts[0].shape[0]
    for side in range(CORES):
        own, after, low, high, before = parts[5 * side : 5 * side + 5]
        column = core if side == 0 else 1 - core

        def start(d):
            return pl.multiple_of((lax.rem(z + d, NZ) * CORES + column) * block, 16)

        whole_ref[pl.ds(start(0), block), :] = own[...].astype(F32)
        whole_ref[pl.ds(start(1), block), :] = after[...].astype(F32)
        whole_ref[pl.ds(start(2), block // 2), :] = low[...].astype(F32)
        whole_ref[pl.ds(start(2) + block // 2, block // 2), :] = high[...].astype(F32)
        whole_ref[pl.ds(start(3), block), :] = before[...].astype(F32)
    out_ref[...] = whole_ref[...].T.astype(BF16)


def mix(capacity, half_ref, route_ref, gate_ref, rows_ref, out_ref):
    one, two = pick_masks(route_ref[...], half_ref[0], capacity)
    rows = rows_ref[...]
    gates = gate_ref[...].T
    out_ref[...] = (
        gates[:, 0:1] * lax.dot_general(as_bf16(one), rows, FIRST, preferred_element_type=F32)
        + gates[:, 1:2] * lax.dot_general(as_bf16(two), rows, FIRST, preferred_element_type=F32)
    ).astype(BF16)


def gather_grad(capacity, half_ref, route_ref, rows_ref, out_ref):
    one, two = pick_masks(route_ref[...], half_ref[0], capacity)
    out_ref[...] = lax.dot_general(as_bf16(one | two), rows_ref[...], FIRST, preferred_element_type=F32).astype(BF16)


def per_device(tokens, cotangent, route_ids, gates, w_gate, w_up, w_down, outer_down, momentum):
    groups = lax.axis_size("expert")
    islands = lax.axis_size("island")
    token_count, top_count = route_ids.shape
    features = tokens.shape[1]
    hidden_count = w_gate.shape[1]
    experts = groups // 2
    capacity = 5 * token_count * top_count // (4 * experts)
    slots = experts * capacity
    half_rows = slots // 2
    n = outer_down.shape[1]
    h = n // 2

    place = lax.axis_index("expert")
    island = lax.axis_index("island")
    xp = ((place % NX) // 2).astype(jnp.int32).reshape(1)
    at = jnp.stack([island // CORES, island % CORES]).astype(jnp.int32)

    pair = [(i, i ^ 1) for i in range(groups)]
    across = [(i, i ^ 3) for i in range(groups)]
    same_x = [[b * NX + x for b in range(N_YZ)] for x in range(NX)]
    other_core = [(i, i ^ 1) for i in range(islands)]
    ahead = [(i, (i + CORES) % islands) for i in range(islands)]
    behind = [(i, (i - CORES) % islands) for i in range(islands)]

    def to_pair(v):
        return lax.ppermute(v, "expert", pair)

    def to_across(v):
        return lax.ppermute(v, "expert", across)

    def by_z(v, perm):
        return lax.ppermute(v, "island", perm)

    def exchange(v):
        v = v.reshape(N_YZ, 2 * capacity, features)
        v = lax.all_to_all(v, "expert", split_axis=0, concat_axis=0, tiled=True, axis_index_groups=same_x)
        return v.reshape(slots, features)

    part = functools.partial
    half_shape = shape(half_rows, features, BF16)
    whole_shape = shape(slots, features, BF16)
    routes, weights = route_ids.T, gates.T

    packed_x = call(part(pack_tokens, capacity), whole_shape, [xp, routes, tokens], smem=1, name="pack_tokens")
    packed_s = call(
        part(pack_scores, capacity),
        whole_shape,
        [xp, routes, weights, cotangent],
        smem=1,
        after=[packed_x],
        name="pack_scores",
    )
    own_x, other_x = call(part(split_rows, capacity), (half_shape,) * 2, [exchange(packed_x)], name="split_x")
    crossed_x = to_across(other_x)
    xs = (own_x, crossed_x, to_pair(own_x), to_pair(crossed_x))
    own_s, other_s = call(
        part(split_rows, capacity), (half_shape,) * 2, [exchange(packed_s)], after=[own_x], name="split_s"
    )
    crossed_s = to_across(other_s)
    ss = (own_s, crossed_s, to_pair(own_s), to_pair(crossed_s))

    total_rows = 2 * slots
    hidden, slope, activated = call(
        forward,
        (
            shape(total_rows, hidden_count, BF16),
            shape(total_rows, hidden_count, F32),
            shape(total_rows, hidden_count, F32),
        ),
        [*xs, w_gate, w_up],
        after=[own_s],
        name="forward",
    )
    outs = call(down, (half_shape,) * 4, [hidden, w_down], after=[ss[2]], name="down")

    half_features = NZ * n
    mine, theirs = call(
        inner_step,
        (shape(half_features, hidden_count, F32), shape(half_features, hidden_count, BF16)),
        [at, *ss, hidden, w_down],
        smem=1,
        after=[outs[0]],
        scratch=[pltpu.VMEM((features, hidden_count), F32)],
        name="inner_step",
    )
    from_core = by_z(theirs, other_core)

    far_ins = call(
        part(backward, 2),
        (half_shape,) * 2,
        [ss[2], ss[3], w_gate, w_up, w_down, slope, activated],
        after=[theirs],
        name="backward_far",
    )
    block32, blockb, halfb = shape(n, hidden_count, F32), shape(n, hidden_count, BF16), shape(h, hidden_count, BF16)
    own_sum, before, after, far_low, far_high = call(
        core_sum, (block32,) * 3 + (halfb,) * 2, [mine, from_core], after=[far_ins[0]], name="core_sum"
    )
    near_ins = call(
        part(backward, 0),
        (half_shape,) * 2,
        [ss[0], ss[1], w_gate, w_up, w_down, slope, activated],
        after=[far_low],
        name="backward_near",
    )

    sum_out = call(add_rows, half_shape, [outs[1], to_pair(outs[3])], after=[near_ins[0]], name="sum_out")
    to_next, to_last = call(
        ring_sum,
        (blockb,) * 2,
        [before, after, by_z(far_low, ahead), by_z(far_high, behind)],
        after=[sum_out],
        name="ring_sum",
    )
    merged_out = call(
        part(merge_rows, capacity),
        whole_shape,
        [outs[0], to_pair(outs[2]), to_across(sum_out)],
        after=[to_next],
        name="merge_out",
    )
    sum_in = call(add_rows, half_shape, [near_ins[1], to_pair(far_ins[1])], after=[merged_out], name="sum_in")
    outer_next, momentum_next, fresh = call(
        part(outer_step, islands),
        (shape(hidden_count, n, F32), shape(hidden_count, n, F32), blockb),
        [own_sum, by_z(to_next, ahead), by_z(to_last, behind), outer_down, momentum],
        after=[sum_in],
        name="outer_step",
    )
    mixed = call(
        part(mix, capacity),
        shape(token_count, features, BF16),
        [xp, routes, weights, exchange(merged_out)],
        smem=1,
        after=[fresh],
        name="mix",
    )
    merged_in = call(
        part(merge_rows, capacity),
        whole_shape,
        [near_ins[0], to_pair(far_ins[0]), to_across(sum_in)],
        after=[mixed],
        name="merge_in",
    )
    left = by_z(fresh, ahead)
    right = by_z(fresh, behind)
    low = by_z(left[:h], ahead)
    high = by_z(right[h:], behind)
    blocks = [fresh, right, low, high, left]
    blocks += [by_z(b, other_core) for b in blocks]
    fresh_down = call(
        assemble,
        shape(hidden_count, features, BF16),
        [at, *blocks],
        smem=1,
        after=[merged_in],
        scratch=[pltpu.VMEM((features, hidden_count), F32)],
        name="assemble",
    )
    input_grad = call(
        part(gather_grad, capacity),
        shape(token_count, features, BF16),
        [xp, routes, exchange(merged_in)],
        smem=1,
        after=[fresh_down],
        name="gather_grad",
    )
    return mixed, input_grad, outer_next, momentum_next, fresh_down


def solution(mesh):
    rows = P(("island", "expert"), None)
    columns = P("expert", "island")
    return jax.shard_map(
        per_device,
        mesh=mesh,
        in_specs=(rows, rows, rows, rows, P("island", "expert"), P("island", "expert"), rows, columns, columns),
        out_specs=(rows, rows, columns, columns, P("expert", None)),
        check_vma=False,
    )
```

```python
import functools

import jax
import jax.numpy as jnp
from jax import lax
from jax.experimental import pallas as pl
from jax.experimental.pallas import tpu as pltpu
from jax.sharding import PartitionSpec as P

NX = 4
N_YZ = 8
CORES = 2
NZ = 4

inner_rate = 0.001
outer_rate = 0.7
outer_beta = 0.9

F32 = jnp.float32
BF16 = jnp.bfloat16
FIRST = (((0,), (0,)), ((), ()))
LAST = (((1,), (1,)), ((), ()))

VMEM = pl.BlockSpec(memory_space=pltpu.VMEM)
SMEM = pl.BlockSpec(memory_space=pltpu.SMEM)


def call(kernel, out_shape, args, smem=0, after=(), scratch=(), name=None, micros=0):
    args, after = list(args), list(after)
    count, skipped = len(args), len(after)

    def body(*refs):
        kernel(*refs[:count], *refs[count + skipped :])

    return pl.pallas_call(
        body,
        out_shape=out_shape,
        in_specs=[SMEM] * smem + [VMEM] * (count - smem) + [pl.BlockSpec(memory_space=pl.ANY)] * skipped,
        out_specs=jax.tree.map(lambda _: VMEM, out_shape),
        scratch_shapes=scratch,
        cost_estimate=pl.CostEstimate(flops=1_150_000_000 * micros, transcendentals=0, bytes_accessed=0),
        compiler_params=pltpu.CompilerParams(vmem_limit_bytes=60 * 1024 * 1024),
        name=name,
    )(*args, *after)


def gate(value, *events):
    return lax.optimization_barrier((value, *events))[0]


def shape(rows, columns, dtype):
    return jax.ShapeDtypeStruct((rows, columns), dtype)


def pick_masks(routes, xp, capacity):
    tokens = routes.shape[1]
    slots = 2 * N_YZ * capacity
    first, second = routes[0:1, :], routes[1:2, :]
    expert = lax.broadcasted_iota(jnp.int32, (2 * N_YZ, tokens), 0)
    named = ((expert == first) | (expert == second)).astype(BF16)
    earlier = (
        lax.broadcasted_iota(jnp.int32, (tokens, tokens), 0)
        < lax.broadcasted_iota(jnp.int32, (tokens, tokens), 1)
    ).astype(BF16)
    before = jnp.dot(named, earlier, preferred_element_type=F32)
    where = lax.broadcasted_iota(jnp.int32, (slots, tokens), 0)

    def mask(ids):
        slot = jnp.sum(jnp.where(expert == ids, before, 0.0), axis=0, keepdims=True).astype(jnp.int32)
        place = (ids >> 1) * (2 * capacity) + jnp.where((ids & 1) == xp, 0, capacity) + slot
        return where == place

    return mask(first), mask(second)


def as_bf16(mask):
    return jnp.where(mask, 1.0, 0.0).astype(BF16)


def pack_tokens(capacity, half_ref, route_ref, tokens_ref, out_ref):
    one, two = pick_masks(route_ref[...], half_ref[0], capacity)
    chosen = jnp.dot(as_bf16(one | two), tokens_ref[...], preferred_element_type=F32)
    out_ref[...] = chosen.astype(BF16)


def pack_scores(capacity, half_ref, route_ref, gate_ref, cotangent_ref, out_ref):
    one, two = pick_masks(route_ref[...], half_ref[0], capacity)
    gates = gate_ref[...]
    weights = jnp.where(one, gates[0:1, :], 0.0) + jnp.where(two, gates[1:2, :], 0.0)
    weight = jnp.sum(weights, axis=1, keepdims=True)
    chosen = jnp.dot(as_bf16(one | two), cotangent_ref[...], preferred_element_type=F32)
    out_ref[...] = (weight * chosen).astype(BF16)


def split_rows(capacity, got_ref, own_ref, other_ref):
    for b in range(N_YZ):
        rows = pl.ds(b * capacity, capacity)
        own_ref[rows, :] = got_ref[pl.ds(2 * b * capacity, capacity), :]
        other_ref[rows, :] = got_ref[pl.ds((2 * b + 1) * capacity, capacity), :]


def merge_rows(capacity, mine_ref, theirs_ref, other_ref, out_ref):
    for b in range(N_YZ):
        rows = pl.ds(b * capacity, capacity)
        whole = mine_ref[rows, :].astype(F32) + theirs_ref[rows, :].astype(F32)
        out_ref[pl.ds(2 * b * capacity, capacity), :] = whole.astype(BF16)
        out_ref[pl.ds((2 * b + 1) * capacity, capacity), :] = other_ref[rows, :]


def add_rows(mine_ref, theirs_ref, out_ref):
    out_ref[...] = (mine_ref[...].astype(F32) + theirs_ref[...].astype(F32)).astype(BF16)


def forward(x0, x1, x2, x3, gate_ref, up_ref, hidden_ref, slope_ref, act_ref):
    rows = x0.shape[0]
    for c, x in enumerate((x0, x1, x2, x3)):
        chunk = pl.ds(c * rows, rows)
        block = x[...]
        gate_pre = jnp.dot(block, gate_ref[...], preferred_element_type=F32)
        up_pre = jnp.dot(block, up_ref[...], preferred_element_type=F32)
        sigmoid_a = jax.nn.sigmoid(gate_pre)
        activated = gate_pre * sigmoid_a
        hidden_ref[chunk, :] = (activated * up_pre).astype(BF16)
        slope_ref[chunk, :] = up_pre * sigmoid_a * (1.0 + gate_pre * (1.0 - sigmoid_a))
        act_ref[chunk, :] = activated


def down(hidden_ref, down_ref, o0, o1, o2, o3):
    rows = o0.shape[0]
    for c, out in enumerate((o0, o1, o2, o3)):
        block = hidden_ref[pl.ds(c * rows, rows), :]
        out[...] = jnp.dot(block, down_ref[...], preferred_element_type=F32).astype(BF16)


def backward(first, *refs):
    count = (len(refs) - 5) // 2
    grads, (gate_ref, up_ref, down_ref, slope_ref, act_ref), outs = refs[:count], refs[count : count + 5], refs[count + 5 :]
    rows = outs[0].shape[0]
    for c, (s, out) in enumerate(zip(grads, outs)):
        chunk = pl.ds((first + c) * rows, rows)
        grad_hidden = lax.dot_general(s[...], down_ref[...], LAST, preferred_element_type=F32)
        grad_gate = (grad_hidden * slope_ref[chunk, :]).astype(BF16)
        grad_up = (grad_hidden * act_ref[chunk, :]).astype(BF16)
        out[...] = (
            lax.dot_general(grad_gate, gate_ref[...], LAST, preferred_element_type=F32)
            + lax.dot_general(grad_up, up_ref[...], LAST, preferred_element_type=F32)
        ).astype(BF16)


def inner_step(place_ref, s0, s1, s2, s3, hidden_ref, down_ref, mine_ref, theirs_ref, whole_ref):
    rows = s0.shape[0]
    total = None
    for c, s in enumerate((s0, s1, s2, s3)):
        part = lax.dot_general(s[...], hidden_ref[pl.ds(c * rows, rows), :], FIRST, preferred_element_type=F32)
        total = part if total is None else total + part
    whole_ref[...] = down_ref[...].astype(F32).T - inner_rate * total
    block = mine_ref.shape[0] // NZ
    z, core = place_ref[0], place_ref[1]
    for d in range(NZ):
        at = lax.rem(z + d, NZ) * CORES
        mine_ref[pl.ds(d * block, block), :] = whole_ref[pl.ds(pl.multiple_of((at + core) * block, 8), block), :]
        theirs_ref[pl.ds(d * block, block), :] = whole_ref[
            pl.ds(pl.multiple_of((at + 1 - core) * block, 8), block), :
        ].astype(BF16)


def core_sum(mine_ref, theirs_ref, own_ref, before_ref, after_ref, far_low_ref, far_high_ref):
    block = own_ref.shape[0]
    half = block // 2

    def total(start, count):
        rows = pl.ds(start, count)
        return mine_ref[rows, :] + theirs_ref[rows, :].astype(F32)

    own_ref[...] = total(0, block)
    after_ref[...] = total(block, block)
    far_low_ref[...] = total(2 * block, half).astype(BF16)
    far_high_ref[...] = total(2 * block + half, half).astype(BF16)
    before_ref[...] = total(3 * block, block)


def ring_sum(before_ref, after_ref, low_ref, high_ref, to_next_ref, to_last_ref):
    half = low_ref.shape[0]
    low, high = pl.ds(0, half), pl.ds(half, half)
    to_next_ref[low, :] = (after_ref[low, :] + low_ref[...].astype(F32)).astype(BF16)
    to_next_ref[high, :] = after_ref[high, :].astype(BF16)
    to_last_ref[low, :] = before_ref[low, :].astype(BF16)
    to_last_ref[high, :] = (before_ref[high, :] + high_ref[...].astype(F32)).astype(BF16)


def outer_step(islands, own_ref, left_ref, right_ref, outer_ref, momentum_ref, next_ref, moved_ref, fresh_ref):
    total = own_ref[...] + left_ref[...].astype(F32) + right_ref[...].astype(F32)
    outer_down = outer_ref[...]
    mean_delta = outer_down - total.T / islands
    momentum_next = outer_beta * momentum_ref[...] + mean_delta
    outer_next = outer_down - outer_rate * (mean_delta + outer_beta * momentum_next)
    next_ref[...] = outer_next
    moved_ref[...] = momentum_next
    fresh_ref[...] = outer_next.T.astype(BF16)


def assemble(place_ref, *refs):
    *parts, out_ref, whole_ref = refs
    z, core = place_ref[0], place_ref[1]
    block = parts[0].shape[0]
    for side in range(CORES):
        own, after, low, high, before = parts[5 * side : 5 * side + 5]
        column = core if side == 0 else 1 - core

        def start(d):
            return pl.multiple_of((lax.rem(z + d, NZ) * CORES + column) * block, 16)

        whole_ref[pl.ds(start(0), block), :] = own[...].astype(F32)
        whole_ref[pl.ds(start(1), block), :] = after[...].astype(F32)
        whole_ref[pl.ds(start(2), block // 2), :] = low[...].astype(F32)
        whole_ref[pl.ds(start(2) + block // 2, block // 2), :] = high[...].astype(F32)
        whole_ref[pl.ds(start(3), block), :] = before[...].astype(F32)
    out_ref[...] = whole_ref[...].T.astype(BF16)


def mix(capacity, half_ref, route_ref, gate_ref, rows_ref, out_ref):
    one, two = pick_masks(route_ref[...], half_ref[0], capacity)
    rows = rows_ref[...]
    gates = gate_ref[...].T
    out_ref[...] = (
        gates[:, 0:1] * lax.dot_general(as_bf16(one), rows, FIRST, preferred_element_type=F32)
        + gates[:, 1:2] * lax.dot_general(as_bf16(two), rows, FIRST, preferred_element_type=F32)
    ).astype(BF16)


def gather_grad(capacity, half_ref, route_ref, rows_ref, out_ref):
    one, two = pick_masks(route_ref[...], half_ref[0], capacity)
    out_ref[...] = lax.dot_general(as_bf16(one | two), rows_ref[...], FIRST, preferred_element_type=F32).astype(BF16)


def per_device(tokens, cotangent, route_ids, gates, w_gate, w_up, w_down, outer_down, momentum):
    groups = lax.axis_size("expert")
    islands = lax.axis_size("island")
    token_count, top_count = route_ids.shape
    features = tokens.shape[1]
    hidden_count = w_gate.shape[1]
    experts = groups // 2
    capacity = 5 * token_count * top_count // (4 * experts)
    slots = experts * capacity
    half_rows = slots // 2
    n = outer_down.shape[1]
    h = n // 2

    place = lax.axis_index("expert")
    island = lax.axis_index("island")
    xp = ((place % NX) // 2).astype(jnp.int32).reshape(1)
    at = jnp.stack([island // CORES, island % CORES]).astype(jnp.int32)

    pair = [(i, i ^ 1) for i in range(groups)]
    across = [(i, i ^ 3) for i in range(groups)]
    same_x = [[b * NX + x for b in range(N_YZ)] for x in range(NX)]
    other_core = [(i, i ^ 1) for i in range(islands)]
    ahead = [(i, (i + CORES) % islands) for i in range(islands)]
    behind = [(i, (i - CORES) % islands) for i in range(islands)]

    def to_pair(v):
        return lax.ppermute(v, "expert", pair)

    def to_across(v):
        return lax.ppermute(v, "expert", across)

    def by_z(v, perm):
        return lax.ppermute(v, "island", perm)

    def exchange(v):
        v = v.reshape(N_YZ, 2 * capacity, features)
        v = lax.all_to_all(v, "expert", split_axis=0, concat_axis=0, tiled=True, axis_index_groups=same_x)
        return v.reshape(slots, features)

    part = functools.partial
    half_shape = shape(half_rows, features, BF16)
    whole_shape = shape(slots, features, BF16)
    routes, weights = route_ids.T, gates.T

    packed_x = call(part(pack_tokens, capacity), whole_shape, [xp, routes, tokens], smem=1, name="pack_tokens")
    packed_s = call(
        part(pack_scores, capacity),
        whole_shape,
        [xp, routes, weights, cotangent],
        smem=1,
        after=[packed_x],
        name="pack_scores",
    )
    own_x, other_x = call(part(split_rows, capacity), (half_shape,) * 2, [exchange(packed_x)], name="split_x")
    crossed_x = to_across(other_x)
    near_x = to_pair(own_x)
    far_x = to_pair(gate(crossed_x, near_x))
    got_s = exchange(gate(packed_s, own_x))
    own_s, other_s = call(
        part(split_rows, capacity), (half_shape,) * 2, [gate(got_s, near_x, crossed_x)], name="split_s"
    )
    crossed_s = to_across(other_s)
    near_s = to_pair(own_s)
    far_s = to_pair(gate(crossed_s, far_x))

    total_rows = 2 * slots
    hidden, slope, activated = call(
        forward,
        (
            shape(total_rows, hidden_count, BF16),
            shape(total_rows, hidden_count, F32),
            shape(total_rows, hidden_count, F32),
        ),
        [own_x, crossed_x, near_x, far_x, w_gate, w_up],
        after=[own_s, crossed_s],
        name="forward",
    )
    outs = call(down, (half_shape,) * 4, [hidden, w_down], name="down")
    far_out = to_pair(gate(outs[3], near_s))
    near_out = to_pair(gate(outs[2], far_s))

    half_features = NZ * n
    mine, theirs = call(
        inner_step,
        (shape(half_features, hidden_count, F32), shape(half_features, hidden_count, BF16)),
        [at, own_s, crossed_s, near_s, far_s, hidden, w_down],
        smem=1,
        after=[outs[0]],
        scratch=[pltpu.VMEM((features, hidden_count), F32)],
        name="inner_step",
        micros=20,
    )
    from_core = by_z(theirs, other_core)

    def back(first, grads, name, after):
        return call(
            part(backward, first),
            (half_shape,) * len(grads),
            [*grads, w_gate, w_up, w_down, slope, activated],
            after=after,
            name=name,
            micros=20,
        )

    far_ins = back(2, [near_s, far_s], "backward_far", [theirs, far_out])
    block32, blockb, halfb = shape(n, hidden_count, F32), shape(n, hidden_count, BF16), shape(h, hidden_count, BF16)
    own_sum, before, after, far_low, far_high = call(
        core_sum, (block32,) * 3 + (halfb,) * 2, [mine, from_core], after=[far_ins[0]], name="core_sum", micros=3
    )

    sum_out = call(add_rows, half_shape, [outs[1], far_out], after=[far_low, near_out], name="sum_out", micros=2)
    across_out = to_across(sum_out)
    far_in = to_pair(gate(far_ins[1], far_out))
    (crossed_in,) = back(1, [crossed_s], "backward_crossed", [sum_out])
    to_next, to_last = call(
        ring_sum,
        (blockb,) * 2,
        [before, after, by_z(far_low, ahead), by_z(far_high, behind)],
        after=[crossed_in],
        name="ring_sum",
        micros=2,
    )
    from_left, from_right = by_z(to_next, ahead), by_z(to_last, behind)
    sum_in = call(add_rows, half_shape, [crossed_in, far_in], after=[to_next], name="sum_in", micros=2)
    across_in = to_across(sum_in)
    near_in = to_pair(gate(far_ins[0], near_out))
    (own_in,) = back(0, [own_s], "backward_own", [sum_in])
    merged_out = call(
        part(merge_rows, capacity),
        whole_shape,
        [outs[0], near_out, across_out],
        after=[own_in],
        name="merge_out",
        micros=0,
    )
    back_out = exchange(merged_out)
    outer_next, momentum_next, fresh = call(
        part(outer_step, islands),
        (shape(hidden_count, n, F32), shape(hidden_count, n, F32), blockb),
        [own_sum, from_left, from_right, outer_down, momentum],
        after=[merged_out, near_in],
        name="outer_step",
        micros=3,
    )
    left, right = by_z(fresh, ahead), by_z(fresh, behind)
    merged_in = call(
        part(merge_rows, capacity),
        whole_shape,
        [own_in, near_in, across_in],
        after=[fresh],
        name="merge_in",
        micros=16,
    )
    back_in = exchange(merged_in)
    mixed = call(
        part(mix, capacity),
        shape(token_count, features, BF16),
        [xp, routes, weights, back_out],
        smem=1,
        after=[merged_in],
        name="mix",
        micros=0,
    )
    left, right = gate(left, mixed), gate(right, mixed)
    low, high = by_z(left[:h], ahead), by_z(right[h:], behind)
    blocks = [fresh, right, low, high, left]
    blocks += [by_z(b, other_core) for b in blocks]
    fresh_down = call(
        assemble,
        shape(hidden_count, features, BF16),
        [at, *blocks],
        smem=1,
        after=[mixed],
        scratch=[pltpu.VMEM((features, hidden_count), F32)],
        name="assemble",
        micros=14,
    )
    input_grad = call(
        part(gather_grad, capacity),
        shape(token_count, features, BF16),
        [xp, routes, back_in],
        smem=1,
        after=[fresh_down],
        name="gather_grad",
        micros=3,
    )
    return mixed, input_grad, outer_next, momentum_next, fresh_down


def solution(mesh):
    rows = P(("island", "expert"), None)
    columns = P("expert", "island")
    return jax.shard_map(
        per_device,
        mesh=mesh,
        in_specs=(rows, rows, rows, rows, P("island", "expert"), P("island", "expert"), rows, columns, columns),
        out_specs=(rows, rows, columns, columns, P("expert", None)),
        check_vma=False,
    )
```

```python
import functools

import jax
import jax.numpy as jnp
from jax import lax
from jax.experimental import pallas as pl
from jax.experimental.pallas import tpu as pltpu
from jax.sharding import PartitionSpec as P

NX = 4
N_YZ = 8
CORES = 2
NZ = 4

inner_rate = 0.001
outer_rate = 0.7
outer_beta = 0.9

F32 = jnp.float32
BF16 = jnp.bfloat16
FIRST = (((0,), (0,)), ((), ()))
LAST = (((1,), (1,)), ((), ()))

VMEM = pl.BlockSpec(memory_space=pltpu.VMEM)
SMEM = pl.BlockSpec(memory_space=pltpu.SMEM)


def call(kernel, out_shape, args, smem=0, after=(), scratch=(), name=None, micros=0):
    args, after = list(args), list(after)
    count, skipped = len(args), len(after)

    def body(*refs):
        kernel(*refs[:count], *refs[count + skipped :])

    return pl.pallas_call(
        body,
        out_shape=out_shape,
        in_specs=[SMEM] * smem + [VMEM] * (count - smem) + [pl.BlockSpec(memory_space=pl.ANY)] * skipped,
        out_specs=jax.tree.map(lambda _: VMEM, out_shape),
        scratch_shapes=scratch,
        cost_estimate=pl.CostEstimate(flops=1_150_000_000 * micros, transcendentals=0, bytes_accessed=0),
        compiler_params=pltpu.CompilerParams(vmem_limit_bytes=60 * 1024 * 1024),
        name=name,
    )(*args, *after)


def gate(value, *events):
    return lax.optimization_barrier((value, *events))[0]


def shape(rows, columns, dtype):
    return jax.ShapeDtypeStruct((rows, columns), dtype)


def pick_masks(routes, xp, capacity):
    tokens = routes.shape[1]
    slots = 2 * N_YZ * capacity
    first, second = routes[0:1, :], routes[1:2, :]
    expert = lax.broadcasted_iota(jnp.int32, (2 * N_YZ, tokens), 0)
    named = ((expert == first) | (expert == second)).astype(BF16)
    earlier = (
        lax.broadcasted_iota(jnp.int32, (tokens, tokens), 0)
        < lax.broadcasted_iota(jnp.int32, (tokens, tokens), 1)
    ).astype(BF16)
    before = jnp.dot(named, earlier, preferred_element_type=F32)
    where = lax.broadcasted_iota(jnp.int32, (slots, tokens), 0)

    def mask(ids):
        slot = jnp.sum(jnp.where(expert == ids, before, 0.0), axis=0, keepdims=True).astype(jnp.int32)
        place = (ids >> 1) * (2 * capacity) + jnp.where((ids & 1) == xp, 0, capacity) + slot
        return where == place

    return mask(first), mask(second)


def as_bf16(mask):
    return jnp.where(mask, 1.0, 0.0).astype(BF16)


def pack_tokens(capacity, half_ref, route_ref, tokens_ref, out_ref):
    one, two = pick_masks(route_ref[...], half_ref[0], capacity)
    chosen = jnp.dot(as_bf16(one | two), tokens_ref[...], preferred_element_type=F32)
    out_ref[...] = chosen.astype(BF16)


def pack_scores(capacity, half_ref, route_ref, gate_ref, cotangent_ref, out_ref):
    one, two = pick_masks(route_ref[...], half_ref[0], capacity)
    gates = gate_ref[...]
    weights = jnp.where(one, gates[0:1, :], 0.0) + jnp.where(two, gates[1:2, :], 0.0)
    weight = jnp.sum(weights, axis=1, keepdims=True)
    chosen = jnp.dot(as_bf16(one | two), cotangent_ref[...], preferred_element_type=F32)
    out_ref[...] = (weight * chosen).astype(BF16)


def split_rows(capacity, got_ref, own_ref, other_ref):
    for b in range(N_YZ):
        rows = pl.ds(b * capacity, capacity)
        own_ref[rows, :] = got_ref[pl.ds(2 * b * capacity, capacity), :]
        other_ref[rows, :] = got_ref[pl.ds((2 * b + 1) * capacity, capacity), :]


def merge_rows(capacity, mine_ref, theirs_ref, other_ref, out_ref):
    for b in range(N_YZ):
        rows = pl.ds(b * capacity, capacity)
        whole = mine_ref[rows, :].astype(F32) + theirs_ref[rows, :].astype(F32)
        out_ref[pl.ds(2 * b * capacity, capacity), :] = whole.astype(BF16)
        out_ref[pl.ds((2 * b + 1) * capacity, capacity), :] = other_ref[rows, :]


def add_rows(mine_ref, theirs_ref, out_ref):
    out_ref[...] = (mine_ref[...].astype(F32) + theirs_ref[...].astype(F32)).astype(BF16)


def turn(*refs):
    half = len(refs) // 2
    for matrix, out in zip(refs[:half], refs[half:]):
        out[...] = matrix[...].T


def forward(count, *refs):
    rows, (gate_ref, up_ref, down_ref), results = refs[:count], refs[count : count + 3], refs[count + 3 :]
    for c, x in enumerate(rows):
        hidden_ref, slope_ref, act_ref, out_ref = results[4 * c : 4 * c + 4]
        block = x[...]
        gate_pre = jnp.dot(block, gate_ref[...], preferred_element_type=F32)
        up_pre = jnp.dot(block, up_ref[...], preferred_element_type=F32)
        sigmoid_a = jax.nn.sigmoid(gate_pre)
        activated = gate_pre * sigmoid_a
        hidden = (activated * up_pre).astype(BF16)
        hidden_ref[...] = hidden
        slope_ref[...] = up_pre * sigmoid_a * (1.0 + gate_pre * (1.0 - sigmoid_a))
        act_ref[...] = activated
        out_ref[...] = jnp.dot(hidden, down_ref[...], preferred_element_type=F32).astype(BF16)


def backward(count, *refs):
    chunks, (gate_ref, up_ref, down_ref), outs = refs[: 3 * count], refs[3 * count : 3 * count + 3], refs[3 * count + 3 :]
    for c, out in enumerate(outs):
        s, slope, act = chunks[3 * c : 3 * c + 3]
        grad_hidden = jnp.dot(s[...], down_ref[...], preferred_element_type=F32)
        grad_gate = (grad_hidden * slope[...]).astype(BF16)
        grad_up = (grad_hidden * act[...]).astype(BF16)
        out[...] = (
            jnp.dot(grad_gate, gate_ref[...], preferred_element_type=F32)
            + jnp.dot(grad_up, up_ref[...], preferred_element_type=F32)
        ).astype(BF16)


def add_rows(mine_ref, theirs_ref, out_ref):
    out_ref[...] = (mine_ref[...].astype(F32) + theirs_ref[...].astype(F32)).astype(BF16)


def inner_step(place_ref, s0, s1, s2, s3, h0, h1, h2, h3, down_ref, mine_ref, theirs_ref, whole_ref):
    total = None
    for s, hidden in ((s0, h0), (s1, h1), (s2, h2), (s3, h3)):
        part = lax.dot_general(s[...], hidden[...], FIRST, preferred_element_type=F32)
        total = part if total is None else total + part
    whole_ref[...] = down_ref[...].astype(F32) - inner_rate * total
    block = mine_ref.shape[0] // NZ
    z, core = place_ref[0], place_ref[1]
    for d in range(NZ):
        at = lax.rem(z + d, NZ) * CORES
        mine_ref[pl.ds(d * block, block), :] = whole_ref[pl.ds(pl.multiple_of((at + core) * block, 8), block), :]
        theirs_ref[pl.ds(d * block, block), :] = whole_ref[
            pl.ds(pl.multiple_of((at + 1 - core) * block, 8), block), :
        ].astype(BF16)


def core_sum(mine_ref, theirs_ref, own_ref, before_ref, after_ref, far_low_ref, far_high_ref):
    block = own_ref.shape[0]
    half = block // 2

    def total(start, count):
        rows = pl.ds(start, count)
        return mine_ref[rows, :] + theirs_ref[rows, :].astype(F32)

    own_ref[...] = total(0, block)
    after_ref[...] = total(block, block)
    far_low_ref[...] = total(2 * block, half).astype(BF16)
    far_high_ref[...] = total(2 * block + half, half).astype(BF16)
    before_ref[...] = total(3 * block, block)


def ring_sum(before_ref, after_ref, low_ref, high_ref, to_next_ref, to_last_ref):
    half = low_ref.shape[0]
    low, high = pl.ds(0, half), pl.ds(half, half)
    to_next_ref[low, :] = (after_ref[low, :] + low_ref[...].astype(F32)).astype(BF16)
    to_next_ref[high, :] = after_ref[high, :].astype(BF16)
    to_last_ref[low, :] = before_ref[low, :].astype(BF16)
    to_last_ref[high, :] = (before_ref[high, :] + high_ref[...].astype(F32)).astype(BF16)


def outer_step(islands, own_ref, left_ref, right_ref, outer_ref, momentum_ref, next_ref, moved_ref, fresh_ref):
    total = own_ref[...] + left_ref[...].astype(F32) + right_ref[...].astype(F32)
    outer_down = outer_ref[...]
    mean_delta = outer_down - total / islands
    momentum_next = outer_beta * momentum_ref[...] + mean_delta
    outer_next = outer_down - outer_rate * (mean_delta + outer_beta * momentum_next)
    next_ref[...] = outer_next
    moved_ref[...] = momentum_next
    fresh_ref[...] = outer_next.astype(BF16)


def assemble(place_ref, *refs):
    *parts, out_ref, whole_ref = refs
    z, core = place_ref[0], place_ref[1]
    block = parts[0].shape[0]
    for side in range(CORES):
        own, after, low, high, before = parts[5 * side : 5 * side + 5]
        column = core if side == 0 else 1 - core

        def start(d):
            return pl.multiple_of((lax.rem(z + d, NZ) * CORES + column) * block, 16)

        whole_ref[pl.ds(start(0), block), :] = own[...].astype(F32)
        whole_ref[pl.ds(start(1), block), :] = after[...].astype(F32)
        whole_ref[pl.ds(start(2), block // 2), :] = low[...].astype(F32)
        whole_ref[pl.ds(start(2) + block // 2, block // 2), :] = high[...].astype(F32)
        whole_ref[pl.ds(start(3), block), :] = before[...].astype(F32)
    out_ref[...] = whole_ref[...].T.astype(BF16)


def mix(capacity, half_ref, route_ref, gate_ref, rows_ref, out_ref):
    one, two = pick_masks(route_ref[...], half_ref[0], capacity)
    rows = rows_ref[...]
    gates = gate_ref[...].T
    out_ref[...] = (
        gates[:, 0:1] * lax.dot_general(as_bf16(one), rows, FIRST, preferred_element_type=F32)
        + gates[:, 1:2] * lax.dot_general(as_bf16(two), rows, FIRST, preferred_element_type=F32)
    ).astype(BF16)


def gather_grad(capacity, half_ref, route_ref, rows_ref, out_ref):
    one, two = pick_masks(route_ref[...], half_ref[0], capacity)
    out_ref[...] = lax.dot_general(as_bf16(one | two), rows_ref[...], FIRST, preferred_element_type=F32).astype(BF16)


def per_device(tokens, cotangent, route_ids, gates, w_gate, w_up, w_down, outer_down, momentum):
    groups = lax.axis_size("expert")
    islands = lax.axis_size("island")
    token_count, top_count = route_ids.shape
    features = tokens.shape[1]
    hidden_count = w_gate.shape[1]
    experts = groups // 2
    capacity = 5 * token_count * top_count // (4 * experts)
    slots = experts * capacity
    half_rows = slots // 2
    n = outer_down.shape[1]
    h = n // 2

    place = lax.axis_index("expert")
    island = lax.axis_index("island")
    xp = ((place % NX) // 2).astype(jnp.int32).reshape(1)
    at = jnp.stack([island // CORES, island % CORES]).astype(jnp.int32)

    pair = [(i, i ^ 1) for i in range(groups)]
    across = [(i, i ^ 3) for i in range(groups)]
    same_x = [[b * NX + x for b in range(N_YZ)] for x in range(NX)]
    other_core = [(i, i ^ 1) for i in range(islands)]
    ahead = [(i, (i + CORES) % islands) for i in range(islands)]
    behind = [(i, (i - CORES) % islands) for i in range(islands)]

    def to_pair(v):
        return lax.ppermute(v, "expert", pair)

    def to_across(v):
        return lax.ppermute(v, "expert", across)

    def by_z(v, perm):
        return lax.ppermute(v, "island", perm)

    def exchange(v):
        v = v.reshape(N_YZ, 2 * capacity, features)
        v = lax.all_to_all(v, "expert", split_axis=0, concat_axis=0, tiled=True, axis_index_groups=same_x)
        return v.reshape(slots, features)

    part = functools.partial
    half_shape = shape(half_rows, features, BF16)
    whole_shape = shape(slots, features, BF16)
    routes, weights = route_ids.T, gates.T

    packed_x = call(part(pack_tokens, capacity), whole_shape, [xp, routes, tokens], smem=1, name="pack_tokens")
    packed_s = call(
        part(pack_scores, capacity),
        whole_shape,
        [xp, routes, weights, cotangent],
        smem=1,
        after=[packed_x],
        name="pack_scores",
    )
    turned = shape(hidden_count, features, BF16)
    gate_turned, up_turned = call(turn, (turned,) * 2, [w_gate, w_up], after=[packed_s], name="turn_gate_up", micros=8)
    own_x, other_x = call(
        part(split_rows, capacity), (half_shape,) * 2, [exchange(packed_x)], after=[up_turned], name="split_x"
    )
    (down_turned,) = call(turn, (shape(features, hidden_count, BF16),), [w_down], after=[own_x], name="turn_down", micros=4)
    crossed_x = to_across(other_x)
    near_x = to_pair(own_x)
    far_x = to_pair(gate(crossed_x, near_x, down_turned))
    got_s = exchange(gate(packed_s, own_x))
    own_s, other_s = call(
        part(split_rows, capacity), (half_shape,) * 2, [gate(got_s, near_x, crossed_x)], name="split_s"
    )
    crossed_s = to_across(other_s)
    near_s = to_pair(own_s)
    far_s = to_pair(gate(crossed_s, far_x))

    unit32, unitb = shape(half_rows, hidden_count, F32), shape(half_rows, hidden_count, BF16)

    def ahead_of(rows, name, after, micros):
        results = call(
            part(forward, len(rows)),
            (unitb, unit32, unit32, half_shape) * len(rows),
            [*rows, w_gate, w_up, w_down],
            after=after,
            name=name,
            micros=micros,
        )
        return [results[4 * c : 4 * c + 4] for c in range(len(rows))]

    chunks = ahead_of([own_x, crossed_x, near_x], "forward_near", [own_s], 10)
    chunks += ahead_of([far_x], "forward_far", [chunks[0][0], crossed_s], 10)
    hiddens, slopes, acts, outs = zip(*chunks)
    far_out = to_pair(gate(outs[3], near_s))
    near_out = to_pair(gate(outs[2], far_s))

    half_features = NZ * n
    mine, theirs = call(
        inner_step,
        (shape(half_features, hidden_count, F32), shape(half_features, hidden_count, BF16)),
        [at, own_s, crossed_s, near_s, far_s, *hiddens, down_turned],
        smem=1,
        after=[outs[3]],
        scratch=[pltpu.VMEM((features, hidden_count), F32)],
        name="inner_step",
        micros=20,
    )
    from_core = by_z(theirs, other_core)
    sum_out = call(add_rows, half_shape, [outs[1], far_out], after=[theirs], name="sum_out", micros=2)
    across_out = to_across(sum_out)

    def back(grads, first, name, after, micros):
        args = [v for c, s in enumerate(grads, first) for v in (s, slopes[c], acts[c])]
        return call(
            part(backward, len(grads)),
            (half_shape,) * len(grads),
            [*args, gate_turned, up_turned, down_turned],
            after=after,
            name=name,
            micros=micros,
        )

    far_ins = back([near_s, far_s], 2, "backward_far", [sum_out], 10)
    far_in = to_pair(gate(far_ins[1], far_out))
    near_in = to_pair(gate(far_ins[0], near_out))
    block32, blockb, halfb = shape(n, hidden_count, F32), shape(n, hidden_count, BF16), shape(h, hidden_count, BF16)
    own_sum, before, after, far_low, far_high = call(
        core_sum,
        (block32,) * 3 + (halfb,) * 2,
        [mine, from_core],
        after=[far_ins[0], near_out],
        name="core_sum",
        micros=3,
    )

    merged_out = call(
        part(merge_rows, capacity),
        whole_shape,
        [outs[0], near_out, across_out],
        after=[far_low],
        name="merge_out",
        micros=0,
    )
    back_out = exchange(merged_out)
    (crossed_in,) = back([crossed_s], 1, "backward_crossed", [merged_out], 12)
    to_next, to_last = call(
        ring_sum,
        (blockb,) * 2,
        [before, after, by_z(far_low, ahead), by_z(far_high, behind)],
        after=[crossed_in],
        name="ring_sum",
        micros=0,
    )
    from_left, from_right = by_z(to_next, ahead), by_z(to_last, behind)
    sum_in = call(add_rows, half_shape, [crossed_in, far_in], after=[to_next], name="sum_in", micros=0)
    across_in = to_across(sum_in)
    (own_in,) = back([own_s], 0, "backward_own", [sum_in], 12)
    mixed = call(
        part(mix, capacity),
        shape(token_count, features, BF16),
        [xp, routes, weights, back_out],
        smem=1,
        after=[own_in],
        name="mix",
        micros=0,
    )
    outer_next, momentum_next, fresh = call(
        part(outer_step, islands),
        (block32, block32, blockb),
        [own_sum, from_left, from_right, outer_down.T, momentum.T],
        after=[mixed],
        name="outer_step",
        micros=0,
    )
    left, right = by_z(fresh, ahead), by_z(fresh, behind)
    merged_in = call(
        part(merge_rows, capacity),
        whole_shape,
        [own_in, near_in, across_in],
        after=[fresh],
        name="merge_in",
        micros=10,
    )
    back_in = exchange(merged_in)
    left, right = gate(left, merged_in), gate(right, merged_in)
    low, high = by_z(left[:h], ahead), by_z(right[h:], behind)
    blocks = [fresh, right, low, high, left]
    blocks += [by_z(b, other_core) for b in blocks]
    fresh_down = call(
        assemble,
        shape(hidden_count, features, BF16),
        [at, *blocks],
        smem=1,
        after=[merged_in],
        scratch=[pltpu.VMEM((features, hidden_count), F32)],
        name="assemble",
        micros=14,
    )
    input_grad = call(
        part(gather_grad, capacity),
        shape(token_count, features, BF16),
        [xp, routes, back_in],
        smem=1,
        after=[fresh_down],
        name="gather_grad",
        micros=3,
    )
    return mixed, input_grad, outer_next.T, momentum_next.T, fresh_down


def solution(mesh):
    rows = P(("island", "expert"), None)
    columns = P("expert", "island")
    return jax.shard_map(
        per_device,
        mesh=mesh,
        in_specs=(rows, rows, rows, rows, P("island", "expert"), P("island", "expert"), rows, columns, columns),
        out_specs=(rows, rows, columns, columns, P("expert", None)),
        check_vma=False,
    )
```

```python
import functools

import jax
import jax.numpy as jnp
from jax import lax
from jax.experimental import pallas as pl
from jax.experimental.pallas import tpu as pltpu
from jax.sharding import PartitionSpec as P

NX = 4
N_YZ = 8
CORES = 2
NZ = 4

inner_rate = 0.001
outer_rate = 0.7
outer_beta = 0.9

F32 = jnp.float32
BF16 = jnp.bfloat16
FIRST = (((0,), (0,)), ((), ()))
LAST = (((1,), (1,)), ((), ()))

VMEM = pl.BlockSpec(memory_space=pltpu.VMEM)
SMEM = pl.BlockSpec(memory_space=pltpu.SMEM)


def call(kernel, out_shape, args, smem=0, after=(), scratch=(), name=None, micros=0):
    args, after = list(args), list(after)
    count, skipped = len(args), len(after)

    def body(*refs):
        kernel(*refs[:count], *refs[count + skipped :])

    return pl.pallas_call(
        body,
        out_shape=out_shape,
        in_specs=[SMEM] * smem + [VMEM] * (count - smem) + [pl.BlockSpec(memory_space=pl.ANY)] * skipped,
        out_specs=jax.tree.map(lambda _: VMEM, out_shape),
        scratch_shapes=scratch,
        cost_estimate=pl.CostEstimate(flops=1_150_000_000 * micros, transcendentals=0, bytes_accessed=0),
        compiler_params=pltpu.CompilerParams(vmem_limit_bytes=25_165_824),
        name=name,
    )(*args, *after)


def gate(value, *events):
    return lax.optimization_barrier((value, *events))[0]


def shape(rows, columns, dtype):
    return jax.ShapeDtypeStruct((rows, columns), dtype)


def pick_masks(routes, xp, capacity):
    tokens = routes.shape[1]
    slots = 2 * N_YZ * capacity
    first, second = routes[0:1, :], routes[1:2, :]
    expert = lax.broadcasted_iota(jnp.int32, (2 * N_YZ, tokens), 0)
    named = ((expert == first) | (expert == second)).astype(BF16)
    earlier = (
        lax.broadcasted_iota(jnp.int32, (tokens, tokens), 0)
        < lax.broadcasted_iota(jnp.int32, (tokens, tokens), 1)
    ).astype(BF16)
    before = jnp.dot(named, earlier, preferred_element_type=F32)
    where = lax.broadcasted_iota(jnp.int32, (slots, tokens), 0)

    def mask(ids):
        slot = jnp.sum(jnp.where(expert == ids, before, 0.0), axis=0, keepdims=True).astype(jnp.int32)
        place = (ids >> 1) * (2 * capacity) + jnp.where((ids & 1) == xp, 0, capacity) + slot
        return where == place

    return mask(first), mask(second)


def as_bf16(mask):
    return jnp.where(mask, 1.0, 0.0).astype(BF16)


def pack_tokens(capacity, half_ref, route_ref, tokens_ref, out_ref):
    one, two = pick_masks(route_ref[...], half_ref[0], capacity)
    chosen = jnp.dot(as_bf16(one | two), tokens_ref[...], preferred_element_type=F32)
    out_ref[...] = chosen.astype(BF16)


def pack_scores(capacity, half_ref, route_ref, gate_ref, cotangent_ref, out_ref):
    one, two = pick_masks(route_ref[...], half_ref[0], capacity)
    gates = gate_ref[...]
    weights = jnp.where(one, gates[0:1, :], 0.0) + jnp.where(two, gates[1:2, :], 0.0)
    weight = jnp.sum(weights, axis=1, keepdims=True)
    chosen = jnp.dot(as_bf16(one | two), cotangent_ref[...], preferred_element_type=F32)
    out_ref[...] = (weight * chosen).astype(BF16)


def split_rows(capacity, got_ref, own_ref, other_ref):
    for b in range(N_YZ):
        rows = pl.ds(b * capacity, capacity)
        own_ref[rows, :] = got_ref[pl.ds(2 * b * capacity, capacity), :]
        other_ref[rows, :] = got_ref[pl.ds((2 * b + 1) * capacity, capacity), :]


def merge_rows(capacity, mine_ref, theirs_ref, other_ref, out_ref):
    for b in range(N_YZ):
        rows = pl.ds(b * capacity, capacity)
        whole = mine_ref[rows, :].astype(F32) + theirs_ref[rows, :].astype(F32)
        out_ref[pl.ds(2 * b * capacity, capacity), :] = whole.astype(BF16)
        out_ref[pl.ds((2 * b + 1) * capacity, capacity), :] = other_ref[rows, :]


def add_rows(mine_ref, theirs_ref, out_ref):
    out_ref[...] = (mine_ref[...].astype(F32) + theirs_ref[...].astype(F32)).astype(BF16)


def turn(*refs):
    half = len(refs) // 2
    for matrix, out in zip(refs[:half], refs[half:]):
        out[...] = matrix[...].T


def forward(count, *refs):
    rows, (gate_ref, up_ref, down_ref), results = refs[:count], refs[count : count + 3], refs[count + 3 :]
    for c, x in enumerate(rows):
        hidden_ref, slope_ref, act_ref, out_ref = results[4 * c : 4 * c + 4]
        block = x[...]
        gate_pre = jnp.dot(block, gate_ref[...], preferred_element_type=F32)
        up_pre = jnp.dot(block, up_ref[...], preferred_element_type=F32)
        sigmoid_a = jax.nn.sigmoid(gate_pre)
        activated = gate_pre * sigmoid_a
        hidden = (activated * up_pre).astype(BF16)
        hidden_ref[...] = hidden
        slope_ref[...] = up_pre * sigmoid_a * (1.0 + gate_pre * (1.0 - sigmoid_a))
        act_ref[...] = activated
        out_ref[...] = jnp.dot(hidden, down_ref[...], preferred_element_type=F32).astype(BF16)


def backward(count, *refs):
    chunks, (gate_ref, up_ref, down_ref), outs = refs[: 3 * count], refs[3 * count : 3 * count + 3], refs[3 * count + 3 :]
    for c, out in enumerate(outs):
        s, slope, act = chunks[3 * c : 3 * c + 3]
        grad_hidden = jnp.dot(s[...], down_ref[...], preferred_element_type=F32)
        grad_gate = (grad_hidden * slope[...]).astype(BF16)
        grad_up = (grad_hidden * act[...]).astype(BF16)
        out[...] = (
            jnp.dot(grad_gate, gate_ref[...], preferred_element_type=F32)
            + jnp.dot(grad_up, up_ref[...], preferred_element_type=F32)
        ).astype(BF16)


def add_rows(mine_ref, theirs_ref, out_ref):
    out_ref[...] = (mine_ref[...].astype(F32) + theirs_ref[...].astype(F32)).astype(BF16)


def inner_step(place_ref, s0, s1, s2, s3, h0, h1, h2, h3, down_ref, mine_ref, theirs_ref, whole_ref):
    total = None
    for s, hidden in ((s0, h0), (s1, h1), (s2, h2), (s3, h3)):
        part = lax.dot_general(s[...], hidden[...], FIRST, preferred_element_type=F32)
        total = part if total is None else total + part
    whole_ref[...] = down_ref[...].astype(F32) - inner_rate * total
    block = mine_ref.shape[0] // NZ
    z, core = place_ref[0], place_ref[1]
    for d in range(NZ):
        at = lax.rem(z + d, NZ) * CORES
        mine_ref[pl.ds(d * block, block), :] = whole_ref[pl.ds(pl.multiple_of((at + core) * block, 8), block), :]
        theirs_ref[pl.ds(d * block, block), :] = whole_ref[
            pl.ds(pl.multiple_of((at + 1 - core) * block, 8), block), :
        ].astype(BF16)


def core_sum(mine_ref, theirs_ref, own_ref, before_ref, after_ref, far_low_ref, far_high_ref):
    block = own_ref.shape[0]
    half = block // 2

    def total(start, count):
        rows = pl.ds(start, count)
        return mine_ref[rows, :] + theirs_ref[rows, :].astype(F32)

    own_ref[...] = total(0, block)
    after_ref[...] = total(block, block)
    far_low_ref[...] = total(2 * block, half).astype(BF16)
    far_high_ref[...] = total(2 * block + half, half).astype(BF16)
    before_ref[...] = total(3 * block, block)


def ring_sum(before_ref, after_ref, low_ref, high_ref, to_next_ref, to_last_ref):
    half = low_ref.shape[0]
    low, high = pl.ds(0, half), pl.ds(half, half)
    to_next_ref[low, :] = (after_ref[low, :] + low_ref[...].astype(F32)).astype(BF16)
    to_next_ref[high, :] = after_ref[high, :].astype(BF16)
    to_last_ref[low, :] = before_ref[low, :].astype(BF16)
    to_last_ref[high, :] = (before_ref[high, :] + high_ref[...].astype(F32)).astype(BF16)


def outer_step(islands, own_ref, left_ref, right_ref, outer_ref, momentum_ref, next_ref, moved_ref, fresh_ref):
    total = own_ref[...] + left_ref[...].astype(F32) + right_ref[...].astype(F32)
    outer_down = outer_ref[...]
    mean_delta = outer_down - total / islands
    momentum_next = outer_beta * momentum_ref[...] + mean_delta
    outer_next = outer_down - outer_rate * (mean_delta + outer_beta * momentum_next)
    next_ref[...] = outer_next
    moved_ref[...] = momentum_next
    fresh_ref[...] = outer_next.astype(BF16)


def assemble(place_ref, *refs):
    *parts, out_ref, whole_ref = refs
    z, core = place_ref[0], place_ref[1]
    block = parts[0].shape[0]
    for side in range(CORES):
        own, after, low, high, before = parts[5 * side : 5 * side + 5]
        column = core if side == 0 else 1 - core

        def start(d):
            return pl.multiple_of((lax.rem(z + d, NZ) * CORES + column) * block, 16)

        whole_ref[pl.ds(start(0), block), :] = own[...].astype(F32)
        whole_ref[pl.ds(start(1), block), :] = after[...].astype(F32)
        whole_ref[pl.ds(start(2), block // 2), :] = low[...].astype(F32)
        whole_ref[pl.ds(start(2) + block // 2, block // 2), :] = high[...].astype(F32)
        whole_ref[pl.ds(start(3), block), :] = before[...].astype(F32)
    out_ref[...] = whole_ref[...].T.astype(BF16)


def mix(capacity, half_ref, route_ref, gate_ref, rows_ref, out_ref):
    one, two = pick_masks(route_ref[...], half_ref[0], capacity)
    rows = rows_ref[...]
    gates = gate_ref[...].T
    out_ref[...] = (
        gates[:, 0:1] * lax.dot_general(as_bf16(one), rows, FIRST, preferred_element_type=F32)
        + gates[:, 1:2] * lax.dot_general(as_bf16(two), rows, FIRST, preferred_element_type=F32)
    ).astype(BF16)


def gather_grad(capacity, half_ref, route_ref, rows_ref, out_ref):
    one, two = pick_masks(route_ref[...], half_ref[0], capacity)
    out_ref[...] = lax.dot_general(as_bf16(one | two), rows_ref[...], FIRST, preferred_element_type=F32).astype(BF16)


def per_device(tokens, cotangent, route_ids, gates, w_gate, w_up, w_down, outer_down, momentum):
    groups = lax.axis_size("expert")
    islands = lax.axis_size("island")
    token_count, top_count = route_ids.shape
    features = tokens.shape[1]
    hidden_count = w_gate.shape[1]
    experts = groups // 2
    capacity = 5 * token_count * top_count // (4 * experts)
    slots = experts * capacity
    half_rows = slots // 2
    n = outer_down.shape[1]
    h = n // 2

    place = lax.axis_index("expert")
    island = lax.axis_index("island")
    xp = ((place % NX) // 2).astype(jnp.int32).reshape(1)
    at = jnp.stack([island // CORES, island % CORES]).astype(jnp.int32)

    pair = [(i, i ^ 1) for i in range(groups)]
    across = [(i, i ^ 3) for i in range(groups)]
    same_x = [[b * NX + x for b in range(N_YZ)] for x in range(NX)]
    other_core = [(i, i ^ 1) for i in range(islands)]
    ahead = [(i, (i + CORES) % islands) for i in range(islands)]
    behind = [(i, (i - CORES) % islands) for i in range(islands)]

    def to_pair(v):
        return lax.ppermute(v, "expert", pair)

    def to_across(v):
        return lax.ppermute(v, "expert", across)

    def by_z(v, perm):
        return lax.ppermute(v, "island", perm)

    def exchange(v):
        v = v.reshape(N_YZ, 2 * capacity, features)
        v = lax.all_to_all(v, "expert", split_axis=0, concat_axis=0, tiled=True, axis_index_groups=same_x)
        return v.reshape(slots, features)

    part = functools.partial
    half_shape = shape(half_rows, features, BF16)
    whole_shape = shape(slots, features, BF16)
    routes, weights = route_ids.T, gates.T

    packed_x = call(part(pack_tokens, capacity), whole_shape, [xp, routes, tokens], smem=1, name="pack_tokens")
    packed_s = call(
        part(pack_scores, capacity),
        whole_shape,
        [xp, routes, weights, cotangent],
        smem=1,
        after=[packed_x],
        name="pack_scores",
    )
    turned = shape(hidden_count, features, BF16)
    gate_turned, up_turned = call(turn, (turned,) * 2, [w_gate, w_up], after=[packed_s], name="turn_gate_up", micros=8)
    own_x, other_x = call(
        part(split_rows, capacity), (half_shape,) * 2, [exchange(packed_x)], after=[up_turned], name="split_x"
    )
    (down_turned,) = call(turn, (shape(features, hidden_count, BF16),), [w_down], after=[own_x], name="turn_down", micros=4)
    crossed_x = to_across(other_x)
    near_x = to_pair(own_x)
    far_x = to_pair(gate(crossed_x, near_x, down_turned))
    got_s = exchange(gate(packed_s, own_x))
    own_s, other_s = call(
        part(split_rows, capacity), (half_shape,) * 2, [gate(got_s, near_x, crossed_x)], name="split_s"
    )
    crossed_s = to_across(other_s)
    near_s = to_pair(own_s)
    far_s = to_pair(gate(crossed_s, far_x))

    unit32, unitb = shape(half_rows, hidden_count, F32), shape(half_rows, hidden_count, BF16)

    def ahead_of(rows, name, after, micros):
        results = call(
            part(forward, len(rows)),
            (unitb, unit32, unit32, half_shape) * len(rows),
            [*rows, w_gate, w_up, w_down],
            after=after,
            name=name,
            micros=micros,
        )
        return [results[4 * c : 4 * c + 4] for c in range(len(rows))]

    chunks = ahead_of([own_x, crossed_x, near_x], "forward_near", [own_s], 10)
    chunks += ahead_of([far_x], "forward_far", [chunks[0][0], crossed_s], 10)
    hiddens, slopes, acts, outs = zip(*chunks)
    far_out = to_pair(gate(outs[3], near_s))
    near_out = to_pair(gate(outs[2], far_s))

    half_features = NZ * n
    mine, theirs = call(
        inner_step,
        (shape(half_features, hidden_count, F32), shape(half_features, hidden_count, BF16)),
        [at, own_s, crossed_s, near_s, far_s, *hiddens, down_turned],
        smem=1,
        after=[outs[3]],
        scratch=[pltpu.VMEM((features, hidden_count), F32)],
        name="inner_step",
        micros=20,
    )
    from_core = by_z(theirs, other_core)
    sum_out = call(add_rows, half_shape, [outs[1], far_out], after=[theirs], name="sum_out", micros=2)
    across_out = to_across(sum_out)

    def back(grads, first, name, after, micros):
        args = [v for c, s in enumerate(grads, first) for v in (s, slopes[c], acts[c])]
        return call(
            part(backward, len(grads)),
            (half_shape,) * len(grads),
            [*args, gate_turned, up_turned, down_turned],
            after=after,
            name=name,
            micros=micros,
        )

    own_in, crossed_in, *far_ins = back([own_s, crossed_s, near_s, far_s], 0, "backward", [sum_out], 10)
    far_in = to_pair(gate(far_ins[1], far_out))
    near_in = to_pair(gate(far_ins[0], near_out))
    block32, blockb, halfb = shape(n, hidden_count, F32), shape(n, hidden_count, BF16), shape(h, hidden_count, BF16)
    own_sum, before, after, far_low, far_high = call(
        core_sum,
        (block32,) * 3 + (halfb,) * 2,
        [mine, from_core],
        after=[far_ins[0], near_out],
        name="core_sum",
        micros=3,
    )

    merged_out = call(
        part(merge_rows, capacity),
        whole_shape,
        [outs[0], near_out, across_out],
        after=[far_low],
        name="merge_out",
        micros=12,
    )
    back_out = exchange(merged_out)
    to_next, to_last = call(
        ring_sum,
        (blockb,) * 2,
        [before, after, by_z(far_low, ahead), by_z(far_high, behind)],
        after=[merged_out],
        name="ring_sum",
        micros=0,
    )
    from_left, from_right = by_z(to_next, ahead), by_z(to_last, behind)
    sum_in = call(add_rows, half_shape, [crossed_in, far_in], after=[to_next], name="sum_in", micros=12, )
    across_in = to_across(sum_in)
    outer_next, momentum_next, fresh = call(
        part(outer_step, islands),
        (block32, block32, blockb),
        [own_sum, from_left, from_right, outer_down.T, momentum.T],
        after=[sum_in],
        name="outer_step",
        micros=0,
    )
    left, right = by_z(fresh, ahead), by_z(fresh, behind)
    merged_in = call(
        part(merge_rows, capacity),
        whole_shape,
        [own_in, near_in, across_in],
        after=[fresh],
        name="merge_in",
        micros=10,
    )
    back_in = exchange(gate(merged_in, back_out))
    mixed = call(
        part(mix, capacity),
        shape(token_count, features, BF16),
        [xp, routes, weights, back_out],
        smem=1,
        after=[merged_in],
        name="mix",
        micros=0,
    )
    left, right = gate(left, merged_in), gate(right, merged_in)
    low, high = by_z(left[:h], ahead), by_z(right[h:], behind)
    blocks = [fresh, right, low, high, left]
    blocks += [by_z(b, other_core) for b in blocks]
    fresh_down = call(
        assemble,
        shape(hidden_count, features, BF16),
        [at, *blocks],
        smem=1,
        after=[mixed],
        scratch=[pltpu.VMEM((features, hidden_count), F32)],
        name="assemble",
        micros=14,
    )
    input_grad = call(
        part(gather_grad, capacity),
        shape(token_count, features, BF16),
        [xp, routes, back_in],
        smem=1,
        after=[fresh_down],
        name="gather_grad",
        micros=3,
    )
    return mixed, input_grad, outer_next.T, momentum_next.T, fresh_down


def solution(mesh):
    rows = P(("island", "expert"), None)
    columns = P("expert", "island")
    return jax.shard_map(
        per_device,
        mesh=mesh,
        in_specs=(rows, rows, rows, rows, P("island", "expert"), P("island", "expert"), rows, columns, columns),
        out_specs=(rows, rows, columns, columns, P("expert", None)),
        check_vma=False,
    )
```

```python
import functools

import jax
import jax.numpy as jnp
from jax import lax
from jax.experimental import pallas as pl
from jax.experimental.pallas import tpu as pltpu
from jax.sharding import PartitionSpec as P

NX = 4
N_YZ = 8
CORES = 2
NZ = 4

inner_rate = 0.001
outer_rate = 0.7
outer_beta = 0.9

F32 = jnp.float32
BF16 = jnp.bfloat16
FIRST = (((0,), (0,)), ((), ()))
LAST = (((1,), (1,)), ((), ()))

VMEM = pl.BlockSpec(memory_space=pltpu.VMEM)
SMEM = pl.BlockSpec(memory_space=pltpu.SMEM)


def call(kernel, out_shape, args, smem=0, after=(), scratch=(), name=None, micros=0):
    args, after = list(args), list(after)
    count, skipped = len(args), len(after)

    def body(*refs):
        kernel(*refs[:count], *refs[count + skipped :])

    return pl.pallas_call(
        body,
        out_shape=out_shape,
        in_specs=[SMEM] * smem + [VMEM] * (count - smem) + [pl.BlockSpec(memory_space=pl.ANY)] * skipped,
        out_specs=jax.tree.map(lambda _: VMEM, out_shape),
        scratch_shapes=scratch,
        cost_estimate=pl.CostEstimate(flops=1_150_000_000 * micros, transcendentals=0, bytes_accessed=0),
        compiler_params=pltpu.CompilerParams(vmem_limit_bytes=24 * 1024 * 1024),
        name=name,
    )(*args, *after)


def gate(value, *events):
    return lax.optimization_barrier((value, *events))[0]


def shape(rows, columns, dtype):
    return jax.ShapeDtypeStruct((rows, columns), dtype)


def pick_masks(routes, xp, capacity):
    tokens = routes.shape[1]
    slots = 2 * N_YZ * capacity
    first, second = routes[0:1, :], routes[1:2, :]
    expert = lax.broadcasted_iota(jnp.int32, (2 * N_YZ, tokens), 0)
    named = ((expert == first) | (expert == second)).astype(BF16)
    earlier = (
        lax.broadcasted_iota(jnp.int32, (tokens, tokens), 0)
        < lax.broadcasted_iota(jnp.int32, (tokens, tokens), 1)
    ).astype(BF16)
    before = jnp.dot(named, earlier, preferred_element_type=F32)
    where = lax.broadcasted_iota(jnp.int32, (slots, tokens), 0)

    def mask(ids):
        slot = jnp.sum(jnp.where(expert == ids, before, 0.0), axis=0, keepdims=True).astype(jnp.int32)
        place = (ids >> 1) * (2 * capacity) + jnp.where((ids & 1) == xp, 0, capacity) + slot
        return where == place

    return mask(first), mask(second)


def as_bf16(mask):
    return jnp.where(mask, 1.0, 0.0).astype(BF16)


def pack_tokens(capacity, half_ref, route_ref, tokens_ref, out_ref):
    one, two = pick_masks(route_ref[...], half_ref[0], capacity)
    chosen = jnp.dot(as_bf16(one | two), tokens_ref[...], preferred_element_type=F32)
    out_ref[...] = chosen.astype(BF16)


def pack_scores(capacity, half_ref, route_ref, gate_ref, cotangent_ref, out_ref):
    one, two = pick_masks(route_ref[...], half_ref[0], capacity)
    gates = gate_ref[...]
    weights = jnp.where(one, gates[0:1, :], 0.0) + jnp.where(two, gates[1:2, :], 0.0)
    weight = jnp.sum(weights, axis=1, keepdims=True)
    chosen = jnp.dot(as_bf16(one | two), cotangent_ref[...], preferred_element_type=F32)
    out_ref[...] = (weight * chosen).astype(BF16)


def split_rows(capacity, got_ref, own_ref, other_ref):
    for b in range(N_YZ):
        rows = pl.ds(b * capacity, capacity)
        own_ref[rows, :] = got_ref[pl.ds(2 * b * capacity, capacity), :]
        other_ref[rows, :] = got_ref[pl.ds((2 * b + 1) * capacity, capacity), :]


def merge_rows(capacity, mine_ref, theirs_ref, other_ref, out_ref):
    for b in range(N_YZ):
        rows = pl.ds(b * capacity, capacity)
        whole = mine_ref[rows, :].astype(F32) + theirs_ref[rows, :].astype(F32)
        out_ref[pl.ds(2 * b * capacity, capacity), :] = whole.astype(BF16)
        out_ref[pl.ds((2 * b + 1) * capacity, capacity), :] = other_ref[rows, :]


def add_rows(mine_ref, theirs_ref, out_ref):
    out_ref[...] = (mine_ref[...].astype(F32) + theirs_ref[...].astype(F32)).astype(BF16)


def turn(*refs):
    half = len(refs) // 2
    for matrix, out in zip(refs[:half], refs[half:]):
        out[...] = matrix[...].T


def forward(count, *refs):
    rows, (gate_ref, up_ref, down_ref), results = refs[:count], refs[count : count + 3], refs[count + 3 :]
    for c, x in enumerate(rows):
        hidden_ref, slope_ref, act_ref, out_ref = results[4 * c : 4 * c + 4]
        block = x[...]
        gate_pre = jnp.dot(block, gate_ref[...], preferred_element_type=F32)
        up_pre = jnp.dot(block, up_ref[...], preferred_element_type=F32)
        sigmoid_a = jax.nn.sigmoid(gate_pre)
        activated = gate_pre * sigmoid_a
        hidden = (activated * up_pre).astype(BF16)
        hidden_ref[...] = hidden
        slope_ref[...] = up_pre * sigmoid_a * (1.0 + gate_pre * (1.0 - sigmoid_a))
        act_ref[...] = activated
        out_ref[...] = jnp.dot(hidden, down_ref[...], preferred_element_type=F32).astype(BF16)


def backward(count, *refs):
    chunks, (gate_ref, up_ref, down_ref), outs = refs[: 3 * count], refs[3 * count : 3 * count + 3], refs[3 * count + 3 :]
    for c, out in enumerate(outs):
        s, slope, act = chunks[3 * c : 3 * c + 3]
        grad_hidden = jnp.dot(s[...], down_ref[...], preferred_element_type=F32)
        grad_gate = (grad_hidden * slope[...]).astype(BF16)
        grad_up = (grad_hidden * act[...]).astype(BF16)
        out[...] = (
            jnp.dot(grad_gate, gate_ref[...], preferred_element_type=F32)
            + jnp.dot(grad_up, up_ref[...], preferred_element_type=F32)
        ).astype(BF16)


def add_rows(mine_ref, theirs_ref, out_ref):
    out_ref[...] = (mine_ref[...].astype(F32) + theirs_ref[...].astype(F32)).astype(BF16)


def inner_step(place_ref, s0, s1, s2, s3, h0, h1, h2, h3, down_ref, mine_ref, theirs_ref, whole_ref):
    total = None
    for s, hidden in ((s0, h0), (s1, h1), (s2, h2), (s3, h3)):
        part = lax.dot_general(s[...], hidden[...], FIRST, preferred_element_type=F32)
        total = part if total is None else total + part
    whole_ref[...] = down_ref[...].astype(F32) - inner_rate * total
    block = mine_ref.shape[0] // NZ
    z, core = place_ref[0], place_ref[1]
    for d in range(NZ):
        at = lax.rem(z + d, NZ) * CORES
        mine_ref[pl.ds(d * block, block), :] = whole_ref[pl.ds(pl.multiple_of((at + core) * block, 8), block), :]
        theirs_ref[pl.ds(d * block, block), :] = whole_ref[
            pl.ds(pl.multiple_of((at + 1 - core) * block, 8), block), :
        ].astype(BF16)


def core_sum(mine_ref, theirs_ref, own_ref, before_ref, after_ref, far_low_ref, far_high_ref):
    block = own_ref.shape[0]
    half = block // 2

    def total(start, count):
        rows = pl.ds(start, count)
        return mine_ref[rows, :] + theirs_ref[rows, :].astype(F32)

    own_ref[...] = total(0, block)
    after_ref[...] = total(block, block)
    far_low_ref[...] = total(2 * block, half).astype(BF16)
    far_high_ref[...] = total(2 * block + half, half).astype(BF16)
    before_ref[...] = total(3 * block, block)


def ring_sum(before_ref, after_ref, low_ref, high_ref, to_next_ref, to_last_ref):
    half = low_ref.shape[0]
    low, high = pl.ds(0, half), pl.ds(half, half)
    to_next_ref[low, :] = (after_ref[low, :] + low_ref[...].astype(F32)).astype(BF16)
    to_next_ref[high, :] = after_ref[high, :].astype(BF16)
    to_last_ref[low, :] = before_ref[low, :].astype(BF16)
    to_last_ref[high, :] = (before_ref[high, :] + high_ref[...].astype(F32)).astype(BF16)


def outer_step(islands, own_ref, left_ref, right_ref, outer_ref, momentum_ref, next_ref, moved_ref, fresh_ref):
    total = own_ref[...] + left_ref[...].astype(F32) + right_ref[...].astype(F32)
    outer_down = outer_ref[...]
    mean_delta = outer_down - total / islands
    momentum_next = outer_beta * momentum_ref[...] + mean_delta
    outer_next = outer_down - outer_rate * (mean_delta + outer_beta * momentum_next)
    next_ref[...] = outer_next
    moved_ref[...] = momentum_next
    fresh_ref[...] = outer_next.astype(BF16)


def assemble(place_ref, *refs):
    *parts, out_ref, whole_ref = refs
    z, core = place_ref[0], place_ref[1]
    block = parts[0].shape[0]
    for side in range(CORES):
        own, after, low, high, before = parts[5 * side : 5 * side + 5]
        column = core if side == 0 else 1 - core

        def start(d):
            return pl.multiple_of((lax.rem(z + d, NZ) * CORES + column) * block, 16)

        whole_ref[pl.ds(start(0), block), :] = own[...].astype(F32)
        whole_ref[pl.ds(start(1), block), :] = after[...].astype(F32)
        whole_ref[pl.ds(start(2), block // 2), :] = low[...].astype(F32)
        whole_ref[pl.ds(start(2) + block // 2, block // 2), :] = high[...].astype(F32)
        whole_ref[pl.ds(start(3), block), :] = before[...].astype(F32)
    out_ref[...] = whole_ref[...].T.astype(BF16)


def mix(capacity, half_ref, route_ref, gate_ref, rows_ref, out_ref):
    one, two = pick_masks(route_ref[...], half_ref[0], capacity)
    rows = rows_ref[...]
    gates = gate_ref[...].T
    out_ref[...] = (
        gates[:, 0:1] * lax.dot_general(as_bf16(one), rows, FIRST, preferred_element_type=F32)
        + gates[:, 1:2] * lax.dot_general(as_bf16(two), rows, FIRST, preferred_element_type=F32)
    ).astype(BF16)


def gather_grad(capacity, half_ref, route_ref, rows_ref, out_ref):
    one, two = pick_masks(route_ref[...], half_ref[0], capacity)
    out_ref[...] = lax.dot_general(as_bf16(one | two), rows_ref[...], FIRST, preferred_element_type=F32).astype(BF16)


def per_device(tokens, cotangent, route_ids, gates, w_gate, w_up, w_down, outer_down, momentum):
    groups = lax.axis_size("expert")
    islands = lax.axis_size("island")
    token_count, top_count = route_ids.shape
    features = tokens.shape[1]
    hidden_count = w_gate.shape[1]
    experts = groups // 2
    capacity = 5 * token_count * top_count // (4 * experts)
    slots = experts * capacity
    half_rows = slots // 2
    n = outer_down.shape[1]
    h = n // 2

    place = lax.axis_index("expert")
    island = lax.axis_index("island")
    xp = ((place % NX) // 2).astype(jnp.int32).reshape(1)
    at = jnp.stack([island // CORES, island % CORES]).astype(jnp.int32)

    pair = [(i, i ^ 1) for i in range(groups)]
    across = [(i, i ^ 3) for i in range(groups)]
    same_x = [[b * NX + x for b in range(N_YZ)] for x in range(NX)]
    other_core = [(i, i ^ 1) for i in range(islands)]
    ahead = [(i, (i + CORES) % islands) for i in range(islands)]
    behind = [(i, (i - CORES) % islands) for i in range(islands)]

    def to_pair(v):
        return lax.ppermute(v, "expert", pair)

    def to_across(v):
        return lax.ppermute(v, "expert", across)

    def by_z(v, perm):
        return lax.ppermute(v, "island", perm)

    def exchange(v):
        v = v.reshape(N_YZ, 2 * capacity, features)
        v = lax.all_to_all(v, "expert", split_axis=0, concat_axis=0, tiled=True, axis_index_groups=same_x)
        return v.reshape(slots, features)

    part = functools.partial
    half_shape = shape(half_rows, features, BF16)
    whole_shape = shape(slots, features, BF16)
    routes, weights = route_ids.T, gates.T

    packed_x = call(part(pack_tokens, capacity), whole_shape, [xp, routes, tokens], smem=1, name="pack_tokens")
    packed_s = call(
        part(pack_scores, capacity),
        whole_shape,
        [xp, routes, weights, cotangent],
        smem=1,
        after=[packed_x],
        name="pack_scores",
    )
    turned = shape(hidden_count, features, BF16)
    gate_turned, up_turned = call(turn, (turned,) * 2, [w_gate, w_up], after=[packed_s], name="turn_gate_up", micros=8)
    own_x, other_x = call(
        part(split_rows, capacity), (half_shape,) * 2, [exchange(packed_x)], after=[up_turned], name="split_x"
    )
    (down_turned,) = call(turn, (shape(features, hidden_count, BF16),), [w_down], after=[own_x], name="turn_down", micros=4)
    crossed_x = to_across(other_x)
    near_x = to_pair(own_x)
    far_x = to_pair(gate(crossed_x, near_x, down_turned))
    got_s = exchange(gate(packed_s, own_x))
    own_s, other_s = call(
        part(split_rows, capacity), (half_shape,) * 2, [gate(got_s, near_x, crossed_x)], name="split_s"
    )
    crossed_s = to_across(other_s)
    near_s = to_pair(own_s)
    far_s = to_pair(gate(crossed_s, far_x))

    unit32, unitb = shape(half_rows, hidden_count, F32), shape(half_rows, hidden_count, BF16)

    def ahead_of(rows, name, after, micros):
        results = call(
            part(forward, len(rows)),
            (unitb, unit32, unit32, half_shape) * len(rows),
            [*rows, w_gate, w_up, w_down],
            after=after,
            name=name,
            micros=micros,
        )
        return [results[4 * c : 4 * c + 4] for c in range(len(rows))]

    chunks = ahead_of([own_x, crossed_x, near_x], "forward_near", [own_s], 10)
    chunks += ahead_of([far_x], "forward_far", [chunks[0][0], crossed_s], 10)
    hiddens, slopes, acts, outs = zip(*chunks)
    far_out = to_pair(gate(outs[3], near_s))
    near_out = to_pair(gate(outs[2], far_s))

    half_features = NZ * n
    mine, theirs = call(
        inner_step,
        (shape(half_features, hidden_count, F32), shape(half_features, hidden_count, BF16)),
        [at, own_s, crossed_s, near_s, far_s, *hiddens, down_turned],
        smem=1,
        after=[outs[3]],
        scratch=[pltpu.VMEM((features, hidden_count), F32)],
        name="inner_step",
        micros=20,
    )
    from_core = by_z(theirs, other_core)
    sum_out = call(add_rows, half_shape, [outs[1], far_out], after=[theirs], name="sum_out", micros=20, )
    across_out = to_across(sum_out)

    def back(grads, first, name, after, micros):
        args = [v for c, s in enumerate(grads, first) for v in (s, slopes[c], acts[c])]
        return call(
            part(backward, len(grads)),
            (half_shape,) * len(grads),
            [*args, gate_turned, up_turned, down_turned],
            after=after,
            name=name,
            micros=micros,
        )

    block32, blockb, halfb = shape(n, hidden_count, F32), shape(n, hidden_count, BF16), shape(h, hidden_count, BF16)
    own_sum, before, after, far_low, far_high = call(
        core_sum,
        (block32,) * 3 + (halfb,) * 2,
        [mine, from_core],
        after=[sum_out],
        name="core_sum",
        micros=0,
    )
    own_in, crossed_in, *far_ins = back([own_s, crossed_s, near_s, far_s], 0, "backward", [far_low], 0)
    far_in = to_pair(gate(far_ins[1], far_out))
    near_in = to_pair(gate(far_ins[0], near_out))

    to_next, to_last = call(
        ring_sum,
        (blockb,) * 2,
        [before, after, by_z(far_low, ahead), by_z(far_high, behind)],
        after=[own_in],
        name="ring_sum",
        micros=0,
    )
    from_left, from_right = by_z(to_next, ahead), by_z(to_last, behind)
    merged_out = call(
        part(merge_rows, capacity),
        whole_shape,
        [outs[0], near_out, across_out],
        after=[to_next],
        name="merge_out",
        micros=8,
    )
    back_out = exchange(merged_out)
    sum_in = call(add_rows, half_shape, [crossed_in, far_in], after=[merged_out], name="sum_in", micros=6, )
    across_in = to_across(sum_in)
    outer_next, momentum_next, fresh = call(
        part(outer_step, islands),
        (block32, block32, blockb),
        [own_sum, from_left, from_right, outer_down.T, momentum.T],
        after=[sum_in],
        name="outer_step",
        micros=3,
    )
    left, right = by_z(fresh, ahead), by_z(fresh, behind)
    merged_in = call(
        part(merge_rows, capacity),
        whole_shape,
        [own_in, near_in, across_in],
        after=[fresh],
        name="merge_in",
        micros=8,
    )
    back_in = exchange(gate(merged_in, back_out))
    mixed = call(
        part(mix, capacity),
        shape(token_count, features, BF16),
        [xp, routes, weights, back_out],
        smem=1,
        after=[merged_in],
        name="mix",
        micros=0,
    )
    left, right = gate(left, merged_in), gate(right, merged_in)
    low, high = by_z(left[:h], ahead), by_z(right[h:], behind)
    blocks = [fresh, right, low, high, left]
    blocks += [by_z(b, other_core) for b in blocks]
    fresh_down = call(
        assemble,
        shape(hidden_count, features, BF16),
        [at, *blocks],
        smem=1,
        after=[mixed],
        scratch=[pltpu.VMEM((features, hidden_count), F32)],
        name="assemble",
        micros=14,
    )
    input_grad = call(
        part(gather_grad, capacity),
        shape(token_count, features, BF16),
        [xp, routes, back_in],
        smem=1,
        after=[fresh_down],
        name="gather_grad",
        micros=3,
    )
    return mixed, input_grad, outer_next.T, momentum_next.T, fresh_down


def solution(mesh):
    rows = P(("island", "expert"), None)
    columns = P("expert", "island")
    return jax.shard_map(
        per_device,
        mesh=mesh,
        in_specs=(rows, rows, rows, rows, P("island", "expert"), P("island", "expert"), rows, columns, columns),
        out_specs=(rows, rows, columns, columns, P("expert", None)),
        check_vma=False,
    )
```

```python
import functools

import jax
import jax.numpy as jnp
from jax import lax
from jax.experimental import pallas as pl
from jax.experimental.pallas import tpu as pltpu
from jax.sharding import PartitionSpec as P

NX = 4
N_YZ = 8
CORES = 2
NZ = 4

inner_rate = 0.001
outer_rate = 0.7
outer_beta = 0.9

F32 = jnp.float32
BF16 = jnp.bfloat16
FIRST = (((0,), (0,)), ((), ()))
LAST = (((1,), (1,)), ((), ()))

VMEM = pl.BlockSpec(memory_space=pltpu.VMEM)
SMEM = pl.BlockSpec(memory_space=pltpu.SMEM)


def call(kernel, out_shape, args, smem=0, after=(), scratch=(), name=None, micros=0):
    args, after = list(args), list(after)
    count, skipped = len(args), len(after)

    def body(*refs):
        kernel(*refs[:count], *refs[count + skipped :])

    return pl.pallas_call(
        body,
        out_shape=out_shape,
        in_specs=[SMEM] * smem + [VMEM] * (count - smem) + [pl.BlockSpec(memory_space=pl.ANY)] * skipped,
        out_specs=jax.tree.map(lambda _: VMEM, out_shape),
        scratch_shapes=scratch,
        cost_estimate=pl.CostEstimate(flops=1_150_000_000 * micros, transcendentals=0, bytes_accessed=0),
        compiler_params=pltpu.CompilerParams(vmem_limit_bytes=24 * 1024 * 1024),
        name=name,
    )(*args, *after)


def gate(value, *events):
    return lax.optimization_barrier((value, *events))[0]


def shape(rows, columns, dtype):
    return jax.ShapeDtypeStruct((rows, columns), dtype)


def pick_masks(routes, xp, capacity):
    tokens = routes.shape[1]
    slots = 2 * N_YZ * capacity
    first, second = routes[0:1, :], routes[1:2, :]
    expert = lax.broadcasted_iota(jnp.int32, (2 * N_YZ, tokens), 0)
    named = ((expert == first) | (expert == second)).astype(BF16)
    earlier = (
        lax.broadcasted_iota(jnp.int32, (tokens, tokens), 0)
        < lax.broadcasted_iota(jnp.int32, (tokens, tokens), 1)
    ).astype(BF16)
    before = jnp.dot(named, earlier, preferred_element_type=F32)
    where = lax.broadcasted_iota(jnp.int32, (slots, tokens), 0)

    def mask(ids):
        slot = jnp.sum(jnp.where(expert == ids, before, 0.0), axis=0, keepdims=True).astype(jnp.int32)
        place = (ids >> 1) * (2 * capacity) + jnp.where((ids & 1) == xp, 0, capacity) + slot
        return where == place

    return mask(first), mask(second)


def as_bf16(mask):
    return jnp.where(mask, 1.0, 0.0).astype(BF16)


def pack_tokens(capacity, half_ref, route_ref, tokens_ref, out_ref):
    one, two = pick_masks(route_ref[...], half_ref[0], capacity)
    chosen = jnp.dot(as_bf16(one | two), tokens_ref[...], preferred_element_type=F32)
    out_ref[...] = chosen.astype(BF16)


def pack_scores(capacity, half_ref, route_ref, gate_ref, cotangent_ref, out_ref):
    one, two = pick_masks(route_ref[...], half_ref[0], capacity)
    gates = gate_ref[...]
    weights = jnp.where(one, gates[0:1, :], 0.0) + jnp.where(two, gates[1:2, :], 0.0)
    weight = jnp.sum(weights, axis=1, keepdims=True)
    chosen = jnp.dot(as_bf16(one | two), cotangent_ref[...], preferred_element_type=F32)
    out_ref[...] = (weight * chosen).astype(BF16)


def split_rows(capacity, got_ref, own_ref, other_ref):
    for b in range(N_YZ):
        rows = pl.ds(b * capacity, capacity)
        own_ref[rows, :] = got_ref[pl.ds(2 * b * capacity, capacity), :]
        other_ref[rows, :] = got_ref[pl.ds((2 * b + 1) * capacity, capacity), :]


def merge_rows(capacity, mine_ref, theirs_ref, other_ref, out_ref):
    for b in range(N_YZ):
        rows = pl.ds(b * capacity, capacity)
        whole = mine_ref[rows, :].astype(F32) + theirs_ref[rows, :].astype(F32)
        out_ref[pl.ds(2 * b * capacity, capacity), :] = whole.astype(BF16)
        out_ref[pl.ds((2 * b + 1) * capacity, capacity), :] = other_ref[rows, :]


def add_rows(mine_ref, theirs_ref, out_ref):
    out_ref[...] = (mine_ref[...].astype(F32) + theirs_ref[...].astype(F32)).astype(BF16)


def turn(*refs):
    half = len(refs) // 2
    for matrix, out in zip(refs[:half], refs[half:]):
        out[...] = matrix[...].T


def forward(count, *refs):
    rows, (gate_ref, up_ref, down_ref), results = refs[:count], refs[count : count + 3], refs[count + 3 :]
    for c, x in enumerate(rows):
        hidden_ref, slope_ref, act_ref, out_ref = results[4 * c : 4 * c + 4]
        block = x[...]
        gate_pre = jnp.dot(block, gate_ref[...], preferred_element_type=F32)
        up_pre = jnp.dot(block, up_ref[...], preferred_element_type=F32)
        sigmoid_a = jax.nn.sigmoid(gate_pre)
        activated = gate_pre * sigmoid_a
        hidden = (activated * up_pre).astype(BF16)
        hidden_ref[...] = hidden
        slope_ref[...] = up_pre * sigmoid_a * (1.0 + gate_pre * (1.0 - sigmoid_a))
        act_ref[...] = activated
        out_ref[...] = jnp.dot(hidden, down_ref[...], preferred_element_type=F32).astype(BF16)


def backward(count, *refs):
    chunks, (gate_ref, up_ref, down_ref), outs = refs[: 3 * count], refs[3 * count : 3 * count + 3], refs[3 * count + 3 :]
    for c, out in enumerate(outs):
        s, slope, act = chunks[3 * c : 3 * c + 3]
        grad_hidden = jnp.dot(s[...], down_ref[...], preferred_element_type=F32)
        grad_gate = (grad_hidden * slope[...]).astype(BF16)
        grad_up = (grad_hidden * act[...]).astype(BF16)
        out[...] = (
            jnp.dot(grad_gate, gate_ref[...], preferred_element_type=F32)
            + jnp.dot(grad_up, up_ref[...], preferred_element_type=F32)
        ).astype(BF16)


def add_rows(mine_ref, theirs_ref, out_ref):
    out_ref[...] = (mine_ref[...].astype(F32) + theirs_ref[...].astype(F32)).astype(BF16)


def inner_step(place_ref, s0, s1, s2, s3, h0, h1, h2, h3, down_ref, mine_ref, theirs_ref, whole_ref):
    total = None
    for s, hidden in ((s0, h0), (s1, h1), (s2, h2), (s3, h3)):
        part = lax.dot_general(s[...], hidden[...], FIRST, preferred_element_type=F32)
        total = part if total is None else total + part
    whole_ref[...] = down_ref[...].astype(F32) - inner_rate * total
    block = mine_ref.shape[0] // NZ
    z, core = place_ref[0], place_ref[1]
    for d in range(NZ):
        at = lax.rem(z + d, NZ) * CORES
        mine_ref[pl.ds(d * block, block), :] = whole_ref[pl.ds(pl.multiple_of((at + core) * block, 8), block), :]
        theirs_ref[pl.ds(d * block, block), :] = whole_ref[
            pl.ds(pl.multiple_of((at + 1 - core) * block, 8), block), :
        ].astype(BF16)


def core_sum(mine_ref, theirs_ref, own_ref, before_ref, after_ref, far_low_ref, far_high_ref):
    block = own_ref.shape[0]
    half = block // 2

    def total(start, count):
        rows = pl.ds(start, count)
        return mine_ref[rows, :] + theirs_ref[rows, :].astype(F32)

    own_ref[...] = total(0, block)
    after_ref[...] = total(block, block)
    far_low_ref[...] = total(2 * block, half).astype(BF16)
    far_high_ref[...] = total(2 * block + half, half).astype(BF16)
    before_ref[...] = total(3 * block, block)


def ring_sum(before_ref, after_ref, low_ref, high_ref, to_next_ref, to_last_ref):
    half = low_ref.shape[0]
    low, high = pl.ds(0, half), pl.ds(half, half)
    to_next_ref[low, :] = (after_ref[low, :] + low_ref[...].astype(F32)).astype(BF16)
    to_next_ref[high, :] = after_ref[high, :].astype(BF16)
    to_last_ref[low, :] = before_ref[low, :].astype(BF16)
    to_last_ref[high, :] = (before_ref[high, :] + high_ref[...].astype(F32)).astype(BF16)


def outer_step(islands, own_ref, left_ref, right_ref, outer_ref, momentum_ref, next_ref, moved_ref, fresh_ref):
    total = own_ref[...] + left_ref[...].astype(F32) + right_ref[...].astype(F32)
    outer_down = outer_ref[...]
    mean_delta = outer_down - total / islands
    momentum_next = outer_beta * momentum_ref[...] + mean_delta
    outer_next = outer_down - outer_rate * (mean_delta + outer_beta * momentum_next)
    next_ref[...] = outer_next
    moved_ref[...] = momentum_next
    fresh_ref[...] = outer_next.astype(BF16)


def assemble(place_ref, *refs):
    *parts, out_ref, whole_ref = refs
    z, core = place_ref[0], place_ref[1]
    block = parts[0].shape[0]
    for side in range(CORES):
        own, after, low, high, before = parts[5 * side : 5 * side + 5]
        column = core if side == 0 else 1 - core

        def start(d):
            return pl.multiple_of((lax.rem(z + d, NZ) * CORES + column) * block, 16)

        whole_ref[pl.ds(start(0), block), :] = own[...]
        whole_ref[pl.ds(start(1), block), :] = after[...]
        whole_ref[pl.ds(start(2), block // 2), :] = low[...]
        whole_ref[pl.ds(start(2) + block // 2, block // 2), :] = high[...]
        whole_ref[pl.ds(start(3), block), :] = before[...]
    out_ref[...] = whole_ref[...].T


def mix(capacity, half_ref, route_ref, gate_ref, rows_ref, out_ref):
    one, two = pick_masks(route_ref[...], half_ref[0], capacity)
    rows = rows_ref[...]
    gates = gate_ref[...].T
    out_ref[...] = (
        gates[:, 0:1] * lax.dot_general(as_bf16(one), rows, FIRST, preferred_element_type=F32)
        + gates[:, 1:2] * lax.dot_general(as_bf16(two), rows, FIRST, preferred_element_type=F32)
    ).astype(BF16)


def gather_grad(capacity, half_ref, route_ref, rows_ref, out_ref):
    one, two = pick_masks(route_ref[...], half_ref[0], capacity)
    out_ref[...] = lax.dot_general(as_bf16(one | two), rows_ref[...], FIRST, preferred_element_type=F32).astype(BF16)


def per_device(tokens, cotangent, route_ids, gates, w_gate, w_up, w_down, outer_down, momentum):
    groups = lax.axis_size("expert")
    islands = lax.axis_size("island")
    token_count, top_count = route_ids.shape
    features = tokens.shape[1]
    hidden_count = w_gate.shape[1]
    experts = groups // 2
    capacity = 5 * token_count * top_count // (4 * experts)
    slots = experts * capacity
    half_rows = slots // 2
    n = outer_down.shape[1]
    h = n // 2

    place = lax.axis_index("expert")
    island = lax.axis_index("island")
    xp = ((place % NX) // 2).astype(jnp.int32).reshape(1)
    at = jnp.stack([island // CORES, island % CORES]).astype(jnp.int32)

    pair = [(i, i ^ 1) for i in range(groups)]
    across = [(i, i ^ 3) for i in range(groups)]
    same_x = [[b * NX + x for b in range(N_YZ)] for x in range(NX)]
    other_core = [(i, i ^ 1) for i in range(islands)]
    ahead = [(i, (i + CORES) % islands) for i in range(islands)]
    behind = [(i, (i - CORES) % islands) for i in range(islands)]

    def to_pair(v):
        return lax.ppermute(v, "expert", pair)

    def to_across(v):
        return lax.ppermute(v, "expert", across)

    def by_z(v, perm):
        return lax.ppermute(v, "island", perm)

    def exchange(v):
        v = v.reshape(N_YZ, 2 * capacity, features)
        v = lax.all_to_all(v, "expert", split_axis=0, concat_axis=0, tiled=True, axis_index_groups=same_x)
        return v.reshape(slots, features)

    part = functools.partial
    half_shape = shape(half_rows, features, BF16)
    whole_shape = shape(slots, features, BF16)
    routes, weights = route_ids.T, gates.T

    packed_x = call(part(pack_tokens, capacity), whole_shape, [xp, routes, tokens], smem=1, name="pack_tokens")
    packed_s = call(
        part(pack_scores, capacity),
        whole_shape,
        [xp, routes, weights, cotangent],
        smem=1,
        after=[packed_x],
        name="pack_scores",
    )
    turned = shape(hidden_count, features, BF16)
    gate_turned, up_turned = call(turn, (turned,) * 2, [w_gate, w_up], after=[packed_s], name="turn_gate_up", micros=8)
    own_x, other_x = call(
        part(split_rows, capacity), (half_shape,) * 2, [exchange(packed_x)], after=[up_turned], name="split_x"
    )
    crossed_x = to_across(other_x)
    near_x = to_pair(own_x)
    far_x = to_pair(gate(crossed_x, near_x))
    (down_turned,) = call(
        turn,
        (shape(features, hidden_count, BF16),),
        [w_down],
        after=[near_x, crossed_x],
        name="turn_down",
        micros=15,
    )
    got_s = exchange(gate(packed_s, own_x))
    own_s, other_s = call(
        part(split_rows, capacity), (half_shape,) * 2, [got_s], after=[down_turned], name="split_s"
    )
    crossed_s = to_across(other_s)
    near_s = to_pair(own_s)
    far_s = to_pair(gate(crossed_s, far_x))

    unit32, unitb = shape(half_rows, hidden_count, F32), shape(half_rows, hidden_count, BF16)

    def ahead_of(rows, name, after, micros):
        results = call(
            part(forward, len(rows)),
            (unitb, unit32, unit32, half_shape) * len(rows),
            [*rows, w_gate, w_up, w_down],
            after=after,
            name=name,
            micros=micros,
        )
        return [results[4 * c : 4 * c + 4] for c in range(len(rows))]

    chunks = ahead_of([own_x, crossed_x, near_x], "forward_near", [own_s], 10)
    chunks += ahead_of([far_x], "forward_far", [chunks[0][0], crossed_s], 10)
    hiddens, slopes, acts, outs = zip(*chunks)
    far_out = to_pair(gate(outs[3], near_s))
    near_out = to_pair(gate(outs[2], far_s))

    half_features = NZ * n
    mine, theirs = call(
        inner_step,
        (shape(half_features, hidden_count, F32), shape(half_features, hidden_count, BF16)),
        [at, own_s, crossed_s, near_s, far_s, *hiddens, down_turned],
        smem=1,
        after=[outs[3]],
        scratch=[pltpu.VMEM((features, hidden_count), F32)],
        name="inner_step",
        micros=20,
    )
    from_core = by_z(theirs, other_core)
    sum_out = call(add_rows, half_shape, [outs[1], far_out], after=[theirs], name="sum_out", micros=20, )
    across_out = to_across(sum_out)

    def back(grads, first, name, after, micros):
        args = [v for c, s in enumerate(grads, first) for v in (s, slopes[c], acts[c])]
        return call(
            part(backward, len(grads)),
            (half_shape,) * len(grads),
            [*args, gate_turned, up_turned, down_turned],
            after=after,
            name=name,
            micros=micros,
        )

    block32, blockb, halfb = shape(n, hidden_count, F32), shape(n, hidden_count, BF16), shape(h, hidden_count, BF16)
    own_sum, before, after, far_low, far_high = call(
        core_sum,
        (block32,) * 3 + (halfb,) * 2,
        [mine, from_core],
        after=[sum_out],
        name="core_sum",
        micros=0,
    )
    own_in, crossed_in, *far_ins = back([own_s, crossed_s, near_s, far_s], 0, "backward", [far_low], 0)
    far_in = to_pair(gate(far_ins[1], far_out))
    near_in = to_pair(gate(far_ins[0], near_out))

    to_next, to_last = call(
        ring_sum,
        (blockb,) * 2,
        [before, after, by_z(far_low, ahead), by_z(far_high, behind)],
        after=[own_in],
        name="ring_sum",
        micros=0,
    )
    from_left, from_right = by_z(to_next, ahead), by_z(to_last, behind)
    merged_out = call(
        part(merge_rows, capacity),
        whole_shape,
        [outs[0], near_out, across_out],
        after=[to_next],
        name="merge_out",
        micros=8,
    )
    back_out = exchange(merged_out)
    sum_in = call(add_rows, half_shape, [crossed_in, far_in], after=[merged_out], name="sum_in", micros=6, )
    across_in = to_across(sum_in)
    outer_next, momentum_next, fresh = call(
        part(outer_step, islands),
        (block32, block32, blockb),
        [own_sum, from_left, from_right, outer_down.T, momentum.T],
        after=[sum_in],
        name="outer_step",
        micros=3,
    )
    left, right = by_z(fresh, ahead), by_z(fresh, behind)
    merged_in = call(
        part(merge_rows, capacity),
        whole_shape,
        [own_in, near_in, across_in],
        after=[fresh],
        name="merge_in",
        micros=8,
    )
    back_in = exchange(gate(merged_in, back_out))
    mixed = call(
        part(mix, capacity),
        shape(token_count, features, BF16),
        [xp, routes, weights, back_out],
        smem=1,
        after=[merged_in],
        name="mix",
        micros=0,
    )
    left, right = gate(left, merged_in), gate(right, merged_in)
    low, high = by_z(left[:h], ahead), by_z(right[h:], behind)
    low, high = gate(low, mixed), gate(high, mixed)
    blocks = [fresh, right, low, high, left]
    blocks += [by_z(b, other_core) for b in blocks]
    fresh_down = call(
        assemble,
        shape(hidden_count, features, BF16),
        [at, *blocks],
        smem=1,
        after=[mixed],
        scratch=[pltpu.VMEM((features, hidden_count), BF16)],
        name="assemble",
        micros=14,
    )
    input_grad = call(
        part(gather_grad, capacity),
        shape(token_count, features, BF16),
        [xp, routes, back_in],
        smem=1,
        after=[fresh_down],
        name="gather_grad",
        micros=3,
    )
    return mixed, input_grad, outer_next.T, momentum_next.T, fresh_down


def solution(mesh):
    rows = P(("island", "expert"), None)
    columns = P("expert", "island")
    return jax.shard_map(
        per_device,
        mesh=mesh,
        in_specs=(rows, rows, rows, rows, P("island", "expert"), P("island", "expert"), rows, columns, columns),
        out_specs=(rows, rows, columns, columns, P("expert", None)),
        check_vma=False,
    )
```

```python
import functools

import jax
import jax.numpy as jnp
from jax import lax
from jax.experimental import pallas as pl
from jax.experimental.pallas import tpu as pltpu
from jax.sharding import PartitionSpec as P

NX = 4
N_YZ = 8
CORES = 2
NZ = 4

inner_rate = 0.001
outer_rate = 0.7
outer_beta = 0.9

F32 = jnp.float32
BF16 = jnp.bfloat16
FIRST = (((0,), (0,)), ((), ()))
LAST = (((1,), (1,)), ((), ()))

VMEM = pl.BlockSpec(memory_space=pltpu.VMEM)
SMEM = pl.BlockSpec(memory_space=pltpu.SMEM)


def call(kernel, out_shape, args, smem=0, after=(), scratch=(), name=None, micros=0):
    args, after = list(args), list(after)
    count, skipped = len(args), len(after)

    def body(*refs):
        kernel(*refs[:count], *refs[count + skipped :])

    return pl.pallas_call(
        body,
        out_shape=out_shape,
        in_specs=[SMEM] * smem + [VMEM] * (count - smem) + [pl.BlockSpec(memory_space=pl.ANY)] * skipped,
        out_specs=jax.tree.map(lambda _: VMEM, out_shape),
        scratch_shapes=scratch,
        cost_estimate=pl.CostEstimate(flops=1_150_000_000 * micros, transcendentals=0, bytes_accessed=0),
        compiler_params=pltpu.CompilerParams(vmem_limit_bytes=24 * 1024 * 1024),
        name=name,
    )(*args, *after)


def gate(value, *events):
    return lax.optimization_barrier((value, *events))[0]


def shape(rows, columns, dtype):
    return jax.ShapeDtypeStruct((rows, columns), dtype)


def pick_masks(routes, xp, capacity):
    tokens = routes.shape[1]
    slots = 2 * N_YZ * capacity
    first, second = routes[0:1, :], routes[1:2, :]
    expert = lax.broadcasted_iota(jnp.int32, (2 * N_YZ, tokens), 0)
    named = ((expert == first) | (expert == second)).astype(BF16)
    earlier = (
        lax.broadcasted_iota(jnp.int32, (tokens, tokens), 0)
        < lax.broadcasted_iota(jnp.int32, (tokens, tokens), 1)
    ).astype(BF16)
    before = jnp.dot(named, earlier, preferred_element_type=F32)
    where = lax.broadcasted_iota(jnp.int32, (slots, tokens), 0)

    def mask(ids):
        slot = jnp.sum(jnp.where(expert == ids, before, 0.0), axis=0, keepdims=True).astype(jnp.int32)
        place = (ids >> 1) * (2 * capacity) + jnp.where((ids & 1) == xp, 0, capacity) + slot
        return where == place

    return mask(first), mask(second)


def as_bf16(mask):
    return jnp.where(mask, 1.0, 0.0).astype(BF16)


def pack_tokens(capacity, half_ref, route_ref, tokens_ref, out_ref):
    one, two = pick_masks(route_ref[...], half_ref[0], capacity)
    chosen = jnp.dot(as_bf16(one | two), tokens_ref[...], preferred_element_type=F32)
    out_ref[...] = chosen.astype(BF16)


def pack_scores(capacity, half_ref, route_ref, gate_ref, cotangent_ref, out_ref):
    one, two = pick_masks(route_ref[...], half_ref[0], capacity)
    gates = gate_ref[...]
    weights = jnp.where(one, gates[0:1, :], 0.0) + jnp.where(two, gates[1:2, :], 0.0)
    weight = jnp.sum(weights, axis=1, keepdims=True)
    chosen = jnp.dot(as_bf16(one | two), cotangent_ref[...], preferred_element_type=F32)
    out_ref[...] = (weight * chosen).astype(BF16)


def split_rows(capacity, got_ref, own_ref, other_ref):
    for b in range(N_YZ):
        rows = pl.ds(b * capacity, capacity)
        own_ref[rows, :] = got_ref[pl.ds(2 * b * capacity, capacity), :]
        other_ref[rows, :] = got_ref[pl.ds((2 * b + 1) * capacity, capacity), :]


def merge_rows(capacity, mine_ref, theirs_ref, other_ref, out_ref):
    for b in range(N_YZ):
        rows = pl.ds(b * capacity, capacity)
        whole = mine_ref[rows, :].astype(F32) + theirs_ref[rows, :].astype(F32)
        out_ref[pl.ds(2 * b * capacity, capacity), :] = whole.astype(BF16)
        out_ref[pl.ds((2 * b + 1) * capacity, capacity), :] = other_ref[rows, :]


def add_rows(mine_ref, theirs_ref, out_ref):
    out_ref[...] = (mine_ref[...].astype(F32) + theirs_ref[...].astype(F32)).astype(BF16)


def turn(*refs):
    half = len(refs) // 2
    for matrix, out in zip(refs[:half], refs[half:]):
        out[...] = matrix[...].T


def forward(count, *refs):
    rows, (gate_ref, up_ref, down_ref), results = refs[:count], refs[count : count + 3], refs[count + 3 :]
    for c, x in enumerate(rows):
        hidden_ref, slope_ref, act_ref, out_ref = results[4 * c : 4 * c + 4]
        block = x[...]
        gate_pre = jnp.dot(block, gate_ref[...], preferred_element_type=F32)
        up_pre = jnp.dot(block, up_ref[...], preferred_element_type=F32)
        sigmoid_a = jax.nn.sigmoid(gate_pre)
        activated = gate_pre * sigmoid_a
        hidden = (activated * up_pre).astype(BF16)
        hidden_ref[...] = hidden
        slope_ref[...] = up_pre * sigmoid_a * (1.0 + gate_pre * (1.0 - sigmoid_a))
        act_ref[...] = activated
        out_ref[...] = jnp.dot(hidden, down_ref[...], preferred_element_type=F32).astype(BF16)


def backward(count, *refs):
    chunks, (gate_ref, up_ref, down_ref), outs = refs[: 3 * count], refs[3 * count : 3 * count + 3], refs[3 * count + 3 :]
    for c, out in enumerate(outs):
        s, slope, act = chunks[3 * c : 3 * c + 3]
        grad_hidden = jnp.dot(s[...], down_ref[...], preferred_element_type=F32)
        grad_gate = (grad_hidden * slope[...]).astype(BF16)
        grad_up = (grad_hidden * act[...]).astype(BF16)
        out[...] = (
            jnp.dot(grad_gate, gate_ref[...], preferred_element_type=F32)
            + jnp.dot(grad_up, up_ref[...], preferred_element_type=F32)
        ).astype(BF16)


def add_rows(mine_ref, theirs_ref, out_ref):
    out_ref[...] = (mine_ref[...].astype(F32) + theirs_ref[...].astype(F32)).astype(BF16)


def inner_step(place_ref, s0, s1, s2, s3, h0, h1, h2, h3, down_ref, mine_ref, theirs_ref, whole_ref):
    total = None
    for s, hidden in ((s0, h0), (s1, h1), (s2, h2), (s3, h3)):
        part = lax.dot_general(s[...], hidden[...], FIRST, preferred_element_type=F32)
        total = part if total is None else total + part
    whole_ref[...] = down_ref[...].astype(F32) - inner_rate * total
    block = mine_ref.shape[0] // NZ
    z, core = place_ref[0], place_ref[1]
    for d in range(NZ):
        at = lax.rem(z + d, NZ) * CORES
        mine_ref[pl.ds(d * block, block), :] = whole_ref[pl.ds(pl.multiple_of((at + core) * block, 8), block), :]
        theirs_ref[pl.ds(d * block, block), :] = whole_ref[
            pl.ds(pl.multiple_of((at + 1 - core) * block, 8), block), :
        ].astype(BF16)


def core_sum(mine_ref, theirs_ref, own_ref, before_ref, after_ref, far_low_ref, far_high_ref):
    block = own_ref.shape[0]
    half = block // 2

    def total(start, count):
        rows = pl.ds(start, count)
        return mine_ref[rows, :] + theirs_ref[rows, :].astype(F32)

    own_ref[...] = total(0, block)
    after_ref[...] = total(block, block)
    far_low_ref[...] = total(2 * block, half).astype(BF16)
    far_high_ref[...] = total(2 * block + half, half).astype(BF16)
    before_ref[...] = total(3 * block, block)


def ring_sum(before_ref, after_ref, low_ref, high_ref, to_next_ref, to_last_ref):
    half = low_ref.shape[0]
    low, high = pl.ds(0, half), pl.ds(half, half)
    to_next_ref[low, :] = (after_ref[low, :] + low_ref[...].astype(F32)).astype(BF16)
    to_next_ref[high, :] = after_ref[high, :].astype(BF16)
    to_last_ref[low, :] = before_ref[low, :].astype(BF16)
    to_last_ref[high, :] = (before_ref[high, :] + high_ref[...].astype(F32)).astype(BF16)


def outer_step(islands, own_ref, left_ref, right_ref, outer_ref, momentum_ref, next_ref, moved_ref, fresh_ref):
    total = own_ref[...] + left_ref[...].astype(F32) + right_ref[...].astype(F32)
    outer_down = outer_ref[...]
    mean_delta = outer_down - total / islands
    momentum_next = outer_beta * momentum_ref[...] + mean_delta
    outer_next = outer_down - outer_rate * (mean_delta + outer_beta * momentum_next)
    next_ref[...] = outer_next
    moved_ref[...] = momentum_next
    fresh_ref[...] = outer_next.astype(BF16)


def assemble(place_ref, *refs):
    *parts, out_ref, whole_ref = refs
    z, core = place_ref[0], place_ref[1]
    block = parts[0].shape[0]
    for side in range(CORES):
        own, after, low, high, before = parts[5 * side : 5 * side + 5]
        column = core if side == 0 else 1 - core

        def start(d):
            return pl.multiple_of((lax.rem(z + d, NZ) * CORES + column) * block, 16)

        whole_ref[pl.ds(start(0), block), :] = own[...]
        whole_ref[pl.ds(start(1), block), :] = after[...]
        whole_ref[pl.ds(start(2), block // 2), :] = low[...]
        whole_ref[pl.ds(start(2) + block // 2, block // 2), :] = high[...]
        whole_ref[pl.ds(start(3), block), :] = before[...]
    out_ref[...] = whole_ref[...].T


def mix(capacity, half_ref, route_ref, gate_ref, rows_ref, out_ref):
    one, two = pick_masks(route_ref[...], half_ref[0], capacity)
    rows = rows_ref[...]
    gates = gate_ref[...].T
    out_ref[...] = (
        gates[:, 0:1] * lax.dot_general(as_bf16(one), rows, FIRST, preferred_element_type=F32)
        + gates[:, 1:2] * lax.dot_general(as_bf16(two), rows, FIRST, preferred_element_type=F32)
    ).astype(BF16)


def gather_grad(capacity, half_ref, route_ref, rows_ref, out_ref):
    one, two = pick_masks(route_ref[...], half_ref[0], capacity)
    out_ref[...] = lax.dot_general(as_bf16(one | two), rows_ref[...], FIRST, preferred_element_type=F32).astype(BF16)


def per_device(tokens, cotangent, route_ids, gates, w_gate, w_up, w_down, outer_down, momentum):
    groups = lax.axis_size("expert")
    islands = lax.axis_size("island")
    token_count, top_count = route_ids.shape
    features = tokens.shape[1]
    hidden_count = w_gate.shape[1]
    experts = groups // 2
    capacity = 5 * token_count * top_count // (4 * experts)
    slots = experts * capacity
    half_rows = slots // 2
    n = outer_down.shape[1]
    h = n // 2

    place = lax.axis_index("expert")
    island = lax.axis_index("island")
    xp = ((place % NX) // 2).astype(jnp.int32).reshape(1)
    at = jnp.stack([island // CORES, island % CORES]).astype(jnp.int32)

    pair = [(i, i ^ 1) for i in range(groups)]
    across = [(i, i ^ 3) for i in range(groups)]
    same_x = [[b * NX + x for b in range(N_YZ)] for x in range(NX)]
    other_core = [(i, i ^ 1) for i in range(islands)]
    ahead = [(i, (i + CORES) % islands) for i in range(islands)]
    behind = [(i, (i - CORES) % islands) for i in range(islands)]

    def to_pair(v):
        return lax.ppermute(v, "expert", pair)

    def to_across(v):
        return lax.ppermute(v, "expert", across)

    def by_z(v, perm):
        return lax.ppermute(v, "island", perm)

    def exchange(v):
        v = v.reshape(N_YZ, 2 * capacity, features)
        v = lax.all_to_all(v, "expert", split_axis=0, concat_axis=0, tiled=True, axis_index_groups=same_x)
        return v.reshape(slots, features)

    part = functools.partial
    half_shape = shape(half_rows, features, BF16)
    whole_shape = shape(slots, features, BF16)
    routes, weights = route_ids.T, gates.T

    packed_x = call(part(pack_tokens, capacity), whole_shape, [xp, routes, tokens], smem=1, name="pack_tokens")
    packed_s = call(
        part(pack_scores, capacity),
        whole_shape,
        [xp, routes, weights, cotangent],
        smem=1,
        after=[packed_x],
        name="pack_scores",
    )
    turned = shape(hidden_count, features, BF16)
    gate_turned, up_turned = call(turn, (turned,) * 2, [w_gate, w_up], after=[packed_s], name="turn_gate_up", micros=8)
    own_x, other_x = call(
        part(split_rows, capacity), (half_shape,) * 2, [exchange(packed_x)], after=[up_turned], name="split_x"
    )
    crossed_x = to_across(other_x)
    near_x = to_pair(own_x)
    far_x = to_pair(gate(crossed_x, near_x))
    (down_turned,) = call(
        turn,
        (shape(features, hidden_count, BF16),),
        [w_down],
        after=[near_x, crossed_x],
        name="turn_down",
        micros=15,
    )
    got_s = exchange(gate(packed_s, own_x))
    own_s, other_s = call(
        part(split_rows, capacity), (half_shape,) * 2, [got_s], after=[down_turned], name="split_s"
    )
    crossed_s = to_across(other_s)
    near_s = to_pair(own_s)
    far_s = to_pair(gate(crossed_s, far_x))

    unit32, unitb = shape(half_rows, hidden_count, F32), shape(half_rows, hidden_count, BF16)

    def ahead_of(rows, name, after, micros):
        results = call(
            part(forward, len(rows)),
            (unitb, unit32, unit32, half_shape) * len(rows),
            [*rows, w_gate, w_up, w_down],
            after=after,
            name=name,
            micros=micros,
        )
        return [results[4 * c : 4 * c + 4] for c in range(len(rows))]

    chunks = ahead_of([own_x, crossed_x, near_x], "forward_near", [own_s], 10)
    chunks += ahead_of([far_x], "forward_far", [chunks[0][0], crossed_s], 10)
    hiddens, slopes, acts, outs = zip(*chunks)
    far_out = to_pair(gate(outs[3], near_s))
    near_out = to_pair(gate(outs[2], far_s))

    half_features = NZ * n
    mine, theirs = call(
        inner_step,
        (shape(half_features, hidden_count, F32), shape(half_features, hidden_count, BF16)),
        [at, own_s, crossed_s, near_s, far_s, *hiddens, down_turned],
        smem=1,
        after=[outs[3]],
        scratch=[pltpu.VMEM((features, hidden_count), F32)],
        name="inner_step",
        micros=20,
    )
    from_core = by_z(theirs, other_core)
    sum_out = call(add_rows, half_shape, [outs[1], far_out], after=[theirs], name="sum_out", micros=20, )
    across_out = to_across(sum_out)

    def back(grads, first, name, after, micros):
        args = [v for c, s in enumerate(grads, first) for v in (s, slopes[c], acts[c])]
        return call(
            part(backward, len(grads)),
            (half_shape,) * len(grads),
            [*args, gate_turned, up_turned, down_turned],
            after=after,
            name=name,
            micros=micros,
        )

    block32, blockb, halfb = shape(n, hidden_count, F32), shape(n, hidden_count, BF16), shape(h, hidden_count, BF16)
    own_sum, before, after, far_low, far_high = call(
        core_sum,
        (block32,) * 3 + (halfb,) * 2,
        [mine, from_core],
        after=[sum_out],
        name="core_sum",
        micros=0,
    )
    own_in, crossed_in, *far_ins = back([own_s, crossed_s, near_s, far_s], 0, "backward", [far_low], 0)
    far_in = to_pair(gate(far_ins[1], far_out))
    near_in = to_pair(gate(far_ins[0], near_out))

    to_next, to_last = call(
        ring_sum,
        (blockb,) * 2,
        [before, after, by_z(far_low, ahead), by_z(far_high, behind)],
        after=[own_in],
        name="ring_sum",
        micros=0,
    )
    from_left, from_right = by_z(to_next, ahead), by_z(to_last, behind)
    merged_out = call(
        part(merge_rows, capacity),
        whole_shape,
        [outs[0], near_out, across_out],
        after=[to_next],
        name="merge_out",
        micros=8,
    )
    back_out = exchange(merged_out)
    sum_in = call(add_rows, half_shape, [crossed_in, far_in], after=[merged_out], name="sum_in", micros=6, )
    across_in = to_across(sum_in)
    outer_next, momentum_next, fresh = call(
        part(outer_step, islands),
        (block32, block32, blockb),
        [own_sum, from_left, from_right, outer_down.T, momentum.T],
        after=[sum_in],
        name="outer_step",
        micros=3,
    )
    left, right = by_z(fresh, ahead), by_z(fresh, behind)
    merged_in = call(
        part(merge_rows, capacity),
        whole_shape,
        [own_in, near_in, across_in],
        after=[fresh],
        name="merge_in",
        micros=8,
    )
    back_in = exchange(gate(merged_in, back_out))
    mixed = call(
        part(mix, capacity),
        shape(token_count, features, BF16),
        [xp, routes, weights, back_out],
        smem=1,
        after=[merged_in],
        name="mix",
        micros=0,
    )
    left, right = gate(left, merged_in), gate(right, merged_in)
    low, high = by_z(left[:h], ahead), by_z(right[h:], behind)
    low, high = gate(low, mixed), gate(high, mixed)
    blocks = [fresh, right, low, high, left]
    blocks += [by_z(b, other_core) for b in blocks]
    fresh_down = call(
        assemble,
        shape(hidden_count, features, BF16),
        [at, *blocks],
        smem=1,
        scratch=[pltpu.VMEM((features, hidden_count), BF16)],
        name="assemble",
        micros=14,
    )
    input_grad = call(
        part(gather_grad, capacity),
        shape(token_count, features, BF16),
        [xp, routes, back_in],
        smem=1,
        after=[blocks[-3]],
        name="gather_grad",
        micros=3,
    )
    return mixed, input_grad, outer_next.T, momentum_next.T, fresh_down


def solution(mesh):
    rows = P(("island", "expert"), None)
    columns = P("expert", "island")
    return jax.shard_map(
        per_device,
        mesh=mesh,
        in_specs=(rows, rows, rows, rows, P("island", "expert"), P("island", "expert"), rows, columns, columns),
        out_specs=(rows, rows, columns, columns, P("expert", None)),
        check_vma=False,
    )
```
